32 devices in a mesh: grp: 2 (over y), chan: 4 (over z), day: 2 (over x), seg: 2 (over core).
Axes of the slice: x: 2, y: 2, z: 4, core: 2. Of those that a mesh axis runs over, the one named last changes fastest.
Arguments:
- records: bfloat16 [4, 4, 512, 2048], P('day', 'seg', ('grp', 'chan')), parts along dimension 2, may hold values from -30 to 30
- visits: int32 [3, 2, 512], P(None, None, ('grp', 'chan')), parts along dimension 2, may hold values from 0 to 63
Outputs:
- correlation: bfloat16 [256, 3, 2, 512], P(('day', 'seg'), None, None, ('grp', 'chan')), parts along dimension 3
The draws below stay inside these ranges and needn't reach their ends.
There are 2 independent parts, one for each index of `grp`. The reference program is written for one: setup_inputs(seed, part) draws one part's arguments, and reference() takes and returns one part's arrays. A program takes and returns all parts, laid end to end along the dimension named above; each array names one. Nothing has to cross between parts.
All inputs are finite; a program needn't handle non-finite values.
Results may differ from the reference program's by a relative error of at most 0.0068.
Values may be sent and summed in bfloat16 or wider, within the bound.
A program may use at most 64 MiB of HBM per device.

```python
import math
import jax
import jax.numpy as jnp
from jax import lax

NS = 2048
FREQS = 512
BAND = 64
LAGS = 256
SEGS = 4
PICKS = 2
CH_DEV = 64
DAY_DEV = 2
BLOCKS = 4
C = 256
DAYS = 4
SEG_DEV = 2
REACH = 1
VISITS = 3
N_DAY = 2
N_SEG = 2


def draw_records(key, part):
    subkeys = jax.random.split(key, 6)
    full_shape = (DAYS, SEGS, C, NS)
    row_shape = (DAYS, SEGS, C, 1)
    tone_bin = jax.random.randint(subkeys[0], row_shape, 0, FREQS)
    sample_index = lax.broadcasted_iota(jnp.int32, full_shape, 3)
    phase_shift = jax.random.uniform(subkeys[1], row_shape, jnp.float32, -math.pi, math.pi)
    amplitude = jax.random.uniform(subkeys[2], row_shape, jnp.float32, 1.0, 3.0)
    tone_wave = amplitude * jnp.sin((tone_bin * sample_index % NS).astype(jnp.float32) * (2.0 * math.pi / NS) + phase_shift)
    noise_part = jnp.clip(jax.random.normal(subkeys[3], full_shape, jnp.float32), -5.0, 5.0)
    row_scale = jnp.exp(jax.random.uniform(subkeys[5], row_shape, jnp.float32, math.log(0.3), math.log(3.0)))
    return (row_scale * (noise_part + tone_wave)).astype(jnp.bfloat16)


def touch_ends(entries, key, low, high):
    dims = entries.shape
    place = [jax.random.randint(jax.random.fold_in(key, axis), (), 0, dims[axis]) for axis in range(len(dims))]
    entries = entries.at[tuple(place)].set(low)
    longest = dims.index(max(dims))
    place[longest] = (place[longest] + 1) % dims[longest]
    return entries.at[tuple(place)].set(high)


def setup_inputs(seed: int = 0, part: int = 0) -> dict:
    splits = jax.random.split(jax.random.key(seed), 3)
    part_keys = jax.random.split(jax.random.fold_in(splits[2], part), 3)
    return {
        "records": draw_records(jax.random.fold_in(jax.random.fold_in(splits[2], part), 71), part),
        "visits": touch_ends(jax.random.randint(part_keys[1], (VISITS, PICKS, C), 0, CH_DEV), jax.random.fold_in(part_keys[1], 1), 0, CH_DEV - 1).astype(jnp.int32),
    }


def forward_table():
    sample_index = lax.broadcasted_iota(jnp.int32, (NS, FREQS), 0)
    freq_index = lax.broadcasted_iota(jnp.int32, (NS, FREQS), 1)
    turns = (sample_index * freq_index % NS).astype(jnp.float32) * (2.0 * math.pi / NS)
    return jnp.concatenate([jnp.cos(turns), -jnp.sin(turns)], 1).astype(jnp.bfloat16)

def inverse_table():
    lag_index = lax.broadcasted_iota(jnp.int32, (LAGS, FREQS), 0) - LAGS // 2
    freq_index = lax.broadcasted_iota(jnp.int32, (LAGS, FREQS), 1)
    turns = (lag_index * freq_index % NS).astype(jnp.float32) * (2.0 * math.pi / NS)
    return jnp.concatenate([jnp.cos(turns), -jnp.sin(turns)], 1).astype(jnp.bfloat16)

def whiten(spectra):
    row_total = spectra.shape[0]
    real_part = spectra[:, :FREQS]
    imag_part = spectra[:, FREQS:]
    band_power = lax.optimization_barrier(jnp.mean((real_part * real_part + imag_part * imag_part).reshape(row_total, FREQS // BAND, BAND), axis=-1)) * 0.5
    factor = jnp.repeat(1.0 / jnp.sqrt(band_power + 1e-06), BAND, axis=1)
    return jnp.concatenate([real_part * factor, imag_part * factor], 1).astype(jnp.bfloat16)

def pair_spectrum(own_block, held_block, picked):
    source_rows = jnp.take(held_block, picked, axis=1)
    own_real = own_block[:, None, :, :FREQS].astype(jnp.float32)
    own_imag = own_block[:, None, :, FREQS:].astype(jnp.float32)
    other_real = source_rows[..., :FREQS].astype(jnp.float32)
    other_imag = source_rows[..., FREQS:].astype(jnp.float32)
    real_sum = lax.optimization_barrier(jnp.sum(own_real * other_real + own_imag * other_imag, axis=0))
    imag_sum = lax.optimization_barrier(jnp.sum(own_real * other_imag - own_imag * other_real, axis=0))
    return jnp.concatenate([real_sum, imag_sum], -1).astype(jnp.bfloat16)

def lag_terms(flat_rows, table_rows):
    return lax.dot_general(table_rows, flat_rows, (((1,), (1,)), ((), ())), preferred_element_type=jnp.float32)

def reference(records, visits):
    table = forward_table()

    def one_day(day_rows):
        spectra = jnp.dot(day_rows.reshape(SEGS * C, NS), table, preferred_element_type=jnp.float32)
        return whiten(spectra).reshape(SEGS, C, 2 * FREQS)
    whitened = lax.map(one_day, records)
    receiver_block = (jnp.arange(C) // CH_DEV).astype(jnp.int32)
    visit_index = jnp.arange(VISITS).astype(jnp.int32)[:, None, None]
    source = ((receiver_block[None, None, :] + REACH - visit_index) % BLOCKS * CH_DEV + visits).astype(jnp.int32)
    inverse = inverse_table()

    def group_term(group, total):
        day_first = (group // N_SEG * DAY_DEV).astype(jnp.int32)
        seg_first = (group % N_SEG * SEG_DEV).astype(jnp.int32)
        zero_index = jnp.zeros((), jnp.int32)
        block = lax.dynamic_slice(whitened, (day_first, seg_first, zero_index, zero_index), (DAY_DEV, SEG_DEV, C, 2 * FREQS))
        block = block.reshape(DAY_DEV * SEG_DEV, C, 2 * FREQS)
        cross_all = lax.map(lambda picked: pair_spectrum(block, block, picked), source)
        return total + lag_terms(cross_all.reshape(-1, 2 * FREQS), inverse)
    total = lax.fori_loop(0, N_DAY * N_SEG, group_term, jnp.zeros((LAGS, VISITS * PICKS * C), jnp.float32))
    scale_factor = 1.0 / math.sqrt(FREQS * DAYS * SEGS)
    return (total * scale_factor).astype(jnp.bfloat16).reshape(LAGS, VISITS, PICKS, C)
```

```python
import functools
import math

import jax
import jax.numpy as jnp
import ml_dtypes
import numpy as np
from jax import lax
from jax.experimental import pallas as pl
from jax.experimental.pallas import tpu as pltpu
from jax.sharding import PartitionSpec as P

FREQS = 512
BAND = 64
LAGS = 256
SEGS = 4
WIDE = 128
CHUNKS = FREQS // WIDE
MESH = pl.DeviceIdType.MESH


def forward_chunks(samples):
    index = np.arange(samples)[:, None] * np.arange(FREQS)[None, :] % samples
    turns = index * (2.0 * math.pi / samples)
    table = np.stack([np.cos(turns), -np.sin(turns)], 1).reshape(samples, 2, CHUNKS, WIDE)
    return table.transpose(2, 0, 1, 3).reshape(CHUNKS, samples, 2 * WIDE).astype(ml_dtypes.bfloat16)


def inverse_chunks(samples):
    index = (np.arange(LAGS) - LAGS // 2)[:, None] * np.arange(FREQS)[None, :] % samples
    turns = index * (2.0 * math.pi / samples)
    table = np.stack([np.cos(turns), -np.sin(turns)], 1).reshape(LAGS, 2, CHUNKS, WIDE)
    return table.transpose(2, 0, 1, 3).reshape(CHUNKS, LAGS, 2 * WIDE).astype(ml_dtypes.bfloat16)


def selector(picks, sets, width):
    pick_count = picks.shape[0]
    across = lax.broadcasted_iota(jnp.int32, (width, width), 1)
    down = lax.broadcasted_iota(jnp.int32, (width, width), 0)
    columns = []
    for p in range(pick_count):
        row = picks[p : p + 1, :].astype(jnp.float32)
        diagonal = jnp.where(across == down, jnp.broadcast_to(row, (width, width)), 0.0)
        columns.append(jnp.sum(diagonal, axis=1, keepdims=True))
    column = jnp.concatenate(columns, 0)
    place = lax.broadcasted_iota(jnp.int32, (pick_count * width, sets * width), 1).astype(jnp.float32)
    rows = [jnp.where(place == column + float(s * width), 1.0, 0.0) for s in range(sets)]
    return jnp.concatenate(rows, 0).astype(jnp.bfloat16)


def whiten(spectra):
    real_part = spectra[:, :WIDE]
    imag_part = spectra[:, WIDE:]
    square = real_part * real_part + imag_part * imag_part
    high = square.astype(jnp.bfloat16)
    low = (square - high.astype(jnp.float32)).astype(jnp.bfloat16)
    down = lax.broadcasted_iota(jnp.int32, (WIDE, WIDE), 0) // BAND
    across = lax.broadcasted_iota(jnp.int32, (WIDE, WIDE), 1) // BAND
    mean = jnp.where(down == across, 0.5 / BAND, 0.0).astype(jnp.bfloat16)
    power = jnp.dot(high, mean, preferred_element_type=jnp.float32)
    power += jnp.dot(low, mean, preferred_element_type=jnp.float32)
    factor = lax.rsqrt(power + 1e-06)
    return jnp.concatenate([real_part * factor, imag_part * factor], 1).astype(jnp.bfloat16)


def cross_spectrum(own, other, select, sets, width):
    picked = jnp.dot(select, other, preferred_element_type=jnp.float32)
    rows = picked.shape[0] // sets
    picks = rows // width
    real_sum = jnp.zeros((rows, WIDE), jnp.float32)
    imag_sum = jnp.zeros((rows, WIDE), jnp.float32)
    for s in range(sets):
        mine = own[s * width : (s + 1) * width].astype(jnp.float32)
        mine = jnp.concatenate([mine] * picks, 0)
        theirs = picked[s * rows : (s + 1) * rows]
        mine_re, mine_im = mine[:, :WIDE], mine[:, WIDE:]
        their_re, their_im = theirs[:, :WIDE], theirs[:, WIDE:]
        real_sum += mine_re * their_re + mine_im * their_im
        imag_sum += mine_re * their_im - mine_im * their_re
    return jnp.concatenate([real_sum, imag_sum], 1).astype(jnp.bfloat16)


def lag_terms(table, cross):
    return lax.dot_general(table, cross, (((1,), (1,)), ((), ())), preferred_element_type=jnp.float32)


def kernel(
    dims, records_hbm, visits, forward_hbm, inverse_hbm, out,
    records, forward, inverse, whitened, held, held_visits, own_select, held_select, terms,
    early_out, late_out, back_out, early_in, late_in, back_in,
    load_sem, table_sem, block_send, block_recv, visit_send, visit_recv,
    early_send, early_recv, late_send, late_recv, back_send, back_recv,
):
    reach, days, segs, blocks, sets, width, picks, scale = dims
    groups = days * segs
    share = LAGS // groups
    cols = picks * width
    chan = lax.axis_index("chan")
    group = lax.axis_index("day") * segs + lax.axis_index("seg")

    def at(offset, step):
        other = lax.rem(group + step, groups)
        return {"chan": lax.rem(chan + offset + blocks, blocks), "day": other // segs, "seg": lax.rem(other, segs)}

    load_records = pltpu.make_async_copy(records_hbm, records, load_sem.at[0])
    load_inverse = pltpu.make_async_copy(inverse_hbm, inverse, load_sem.at[1])
    load_table = [
        pltpu.make_async_copy(forward_hbm.at[c], forward.at[c], table_sem.at[c]) for c in range(CHUNKS)
    ]
    load_records.start()
    load_table[0].start()

    barrier = pltpu.get_barrier_semaphore()
    partners = [(o, k) for o in range(-reach, reach + 1) for k in range(groups) if (o, k) != (0, 0)]
    for o, k in partners:
        pl.semaphore_signal(barrier, inc=1, device_id=at(o, k), device_id_type=MESH)
    for c in range(1, CHUNKS):
        load_table[c].start()
    load_inverse.start()

    for o in range(reach + 1):
        own_select[o] = selector(visits[reach + o], sets, width)

    send_visits, send_blocks = [], []
    load_records.wait()
    for c in range(CHUNKS):
        load_table[c].wait()
        spectra = jnp.dot(records[...], forward[c], preferred_element_type=jnp.float32)
        whitened[c] = whiten(spectra)
        if c == 0:
            pl.semaphore_wait(barrier, len(partners))
            for o in range(1, reach + 1):
                copy = pltpu.make_async_remote_copy(
                    visits.at[reach - o], held_visits.at[o - 1], visit_send.at[o - 1], visit_recv.at[o - 1],
                    device_id=at(o, 0), device_id_type=MESH,
                )
                copy.start()
                send_visits.append(copy)
        for o in range(1, reach + 1):
            copy = pltpu.make_async_remote_copy(
                whitened.at[c], held.at[o - 1, c], block_send.at[o - 1, c], block_recv.at[o - 1, c],
                device_id=at(o, 0), device_id_type=MESH,
            )
            copy.start()
            send_blocks.append(copy)
        if c == 0:
            load_inverse.wait()
        mine = whitened[c]
        cross = cross_spectrum(mine, mine, own_select[0], sets, width)
        part = lag_terms(inverse[c], cross).reshape(groups, share, cols)
        terms[reach] = part if c == 0 else terms[reach] + part

    early_out[...] = terms[reach].astype(jnp.bfloat16)
    send_results = []

    def send_result(source, target, send, recv, offset, step):
        other = lax.rem(group + step, groups)
        copy = pltpu.make_async_remote_copy(
            source.at[other], target.at[step], send.at[step], recv.at[step],
            device_id=at(offset, step), device_id_type=MESH,
        )
        copy.start()
        send_results.append(copy)

    for k in range(1, groups):
        send_result(early_out, early_in, early_send, early_recv, 0, k)

    for o in range(1, reach + 1):
        send_visits[o - 1].wait_recv()
        held_select[o - 1] = selector(held_visits[o - 1], sets, width)

    for c in range(CHUNKS):
        for o in range(1, reach + 1):
            send_blocks[c * reach + o - 1].wait_recv()
            mine, theirs = whitened[c], held[o - 1, c]
            down = cross_spectrum(mine, theirs, own_select[o], sets, width)
            up = cross_spectrum(theirs, mine, held_select[o - 1], sets, width)
            part = lag_terms(inverse[c], jnp.concatenate([down, up], 0))
            for place, piece in ((reach + o, part[:, :cols]), (reach - o, part[:, cols:])):
                piece = piece.reshape(groups, share, cols)
                terms[place] = piece if c == 0 else terms[place] + piece

    for o in range(1, reach + 1):
        back_out[o - 1] = terms[reach - o].astype(jnp.bfloat16)
        for k in range(groups):
            send_result(back_out.at[o - 1], back_in.at[o - 1], back_send.at[o - 1], back_recv.at[o - 1], -o, k)
        late_out[:, :, (o - 1) * cols : o * cols] = terms[reach + o].astype(jnp.bfloat16)
    for k in range(1, groups):
        send_result(late_out, late_in, late_send, late_recv, 0, k)

    for copy in send_results:
        copy.wait_recv()
    total = terms[reach, group]
    for k in range(1, groups):
        total += early_in[k].astype(jnp.float32)
    out[:, reach * cols : (reach + 1) * cols] = (total * scale).astype(jnp.bfloat16)
    for o in range(1, reach + 1):
        total = back_in[o - 1, 0].astype(jnp.float32)
        for k in range(1, groups):
            total += back_in[o - 1, k].astype(jnp.float32)
        out[:, (reach - o) * cols : (reach - o + 1) * cols] = (total * scale).astype(jnp.bfloat16)
        total = terms[reach + o, group]
        for k in range(1, groups):
            total += late_in[k, :, (o - 1) * cols : o * cols].astype(jnp.float32)
        out[:, (reach + o) * cols : (reach + o + 1) * cols] = (total * scale).astype(jnp.bfloat16)
    for copy in send_visits + send_blocks + send_results:
        copy.wait_send()


def local(records, visits):
    day_local, seg_local, width, samples = records.shape
    visit_count, picks, _ = visits.shape
    days, segs, blocks = lax.axis_size("day"), lax.axis_size("seg"), lax.axis_size("chan")
    reach = blocks // 4
    groups = days * segs
    share = LAGS // groups
    sets = day_local * seg_local
    rows = sets * width
    cols = picks * width
    scale = 1.0 / math.sqrt(FREQS * day_local * days * SEGS)
    bf16, f32 = jnp.bfloat16, jnp.float32
    hbm = pl.BlockSpec(memory_space=pl.ANY)
    vmem = pl.BlockSpec(memory_space=pltpu.VMEM)
    dma = pltpu.SemaphoreType.DMA
    flops = 2 * rows * samples * 2 * FREQS + 2 * LAGS * 2 * FREQS * visit_count * cols
    result = pl.pallas_call(
        functools.partial(kernel, (reach, days, segs, blocks, sets, width, picks, scale)),
        out_shape=jax.ShapeDtypeStruct((share, visit_count * cols), bf16),
        in_specs=[hbm, vmem, hbm, hbm],
        out_specs=vmem,
        scratch_shapes=[
            pltpu.VMEM((rows, samples), bf16),
            pltpu.VMEM((CHUNKS, samples, 2 * WIDE), bf16),
            pltpu.VMEM((CHUNKS, LAGS, 2 * WIDE), bf16),
            pltpu.VMEM((CHUNKS, rows, 2 * WIDE), bf16),
            pltpu.VMEM((reach, CHUNKS, rows, 2 * WIDE), bf16),
            pltpu.VMEM((reach, picks, width), jnp.int32),
            pltpu.VMEM((reach + 1, sets * cols, rows), bf16),
            pltpu.VMEM((reach, sets * cols, rows), bf16),
            pltpu.VMEM((visit_count, groups, share, cols), f32),
            pltpu.VMEM((groups, share, cols), bf16),
            pltpu.VMEM((groups, share, reach * cols), bf16),
            pltpu.VMEM((reach, groups, share, cols), bf16),
            pltpu.VMEM((groups, share, cols), bf16),
            pltpu.VMEM((groups, share, reach * cols), bf16),
            pltpu.VMEM((reach, groups, share, cols), bf16),
            dma((2,)), dma((CHUNKS,)), dma((reach, CHUNKS)), dma((reach, CHUNKS)), dma((reach,)), dma((reach,)),
            dma((groups,)), dma((groups,)), dma((groups,)), dma((groups,)),
            dma((reach, groups)), dma((reach, groups)),
        ],
        compiler_params=pltpu.CompilerParams(
            collective_id=0, has_side_effects=True, vmem_limit_bytes=48 * 1024 * 1024
        ),
        cost_estimate=pl.CostEstimate(flops=flops, bytes_accessed=8 * 1024 * 1024, transcendentals=0),
        name="correlate",
    )(records.reshape(rows, samples), visits, forward_chunks(samples), inverse_chunks(samples))
    return result.reshape(share, visit_count, picks, width)


def solution(mesh):
    in_specs = (P("day", "seg", ("grp", "chan"), None), P(None, None, ("grp", "chan")))
    out_specs = P(("day", "seg"), None, None, ("grp", "chan"))
    return jax.shard_map(local, mesh=mesh, in_specs=in_specs, out_specs=out_specs, check_vma=False)
```

```python
import functools
import math

import jax
import jax.numpy as jnp
import ml_dtypes
import numpy as np
from jax import lax
from jax.experimental import pallas as pl
from jax.experimental.pallas import tpu as pltpu
from jax.sharding import PartitionSpec as P

FREQS = 512
BAND = 64
LAGS = 256
SEGS = 4
WIDE = 128
CHUNKS = FREQS // WIDE
MESH = pl.DeviceIdType.MESH


def forward_chunks(samples):
    index = np.arange(samples)[:, None] * np.arange(FREQS)[None, :] % samples
    turns = index * (2.0 * math.pi / samples)
    table = np.stack([np.cos(turns), -np.sin(turns)], 1).reshape(samples, 2, CHUNKS, WIDE)
    return table.transpose(2, 0, 1, 3).reshape(CHUNKS, samples, 2 * WIDE).astype(ml_dtypes.bfloat16)


def inverse_chunks(samples):
    index = (np.arange(LAGS) - LAGS // 2)[:, None] * np.arange(FREQS)[None, :] % samples
    turns = index * (2.0 * math.pi / samples)
    table = np.stack([np.cos(turns), -np.sin(turns)], 1).reshape(LAGS, 2, CHUNKS, WIDE)
    return table.transpose(2, 0, 1, 3).reshape(CHUNKS, LAGS, 2 * WIDE).astype(ml_dtypes.bfloat16)


def selector(picks, sets, width):
    pick_count = picks.shape[0]
    across = lax.broadcasted_iota(jnp.int32, (width, width), 1)
    down = lax.broadcasted_iota(jnp.int32, (width, width), 0)
    columns = []
    for p in range(pick_count):
        row = picks[p : p + 1, :].astype(jnp.float32)
        diagonal = jnp.where(across == down, jnp.broadcast_to(row, (width, width)), 0.0)
        columns.append(jnp.sum(diagonal, axis=1, keepdims=True))
    column = jnp.concatenate(columns, 0)
    place = lax.broadcasted_iota(jnp.int32, (pick_count * width, sets * width), 1).astype(jnp.float32)
    rows = [jnp.where(place == column + float(s * width), 1.0, 0.0) for s in range(sets)]
    return jnp.concatenate(rows, 0).astype(jnp.bfloat16)


def whiten(spectra):
    real_part = spectra[:, :WIDE]
    imag_part = spectra[:, WIDE:]
    square = real_part * real_part + imag_part * imag_part
    high = square.astype(jnp.bfloat16)
    low = (square - high.astype(jnp.float32)).astype(jnp.bfloat16)
    down = lax.broadcasted_iota(jnp.int32, (WIDE, WIDE), 0) // BAND
    across = lax.broadcasted_iota(jnp.int32, (WIDE, WIDE), 1) // BAND
    mean = jnp.where(down == across, 0.5 / BAND, 0.0).astype(jnp.bfloat16)
    power = jnp.dot(high, mean, preferred_element_type=jnp.float32)
    power += jnp.dot(low, mean, preferred_element_type=jnp.float32)
    factor = lax.rsqrt(power + 1e-06)
    return jnp.concatenate([real_part * factor, imag_part * factor], 1).astype(jnp.bfloat16)


def cross_spectrum(own, other, select, sets, width):
    picked = jnp.dot(select, other, preferred_element_type=jnp.float32)
    rows = picked.shape[0] // sets
    picks = rows // width
    real_sum = jnp.zeros((rows, WIDE), jnp.float32)
    imag_sum = jnp.zeros((rows, WIDE), jnp.float32)
    for s in range(sets):
        mine = own[s * width : (s + 1) * width].astype(jnp.float32)
        mine = jnp.concatenate([mine] * picks, 0)
        theirs = picked[s * rows : (s + 1) * rows]
        mine_re, mine_im = mine[:, :WIDE], mine[:, WIDE:]
        their_re, their_im = theirs[:, :WIDE], theirs[:, WIDE:]
        real_sum += mine_re * their_re + mine_im * their_im
        imag_sum += mine_re * their_im - mine_im * their_re
    return jnp.concatenate([real_sum, imag_sum], 1).astype(jnp.bfloat16)


def lag_terms(table, cross):
    return lax.dot_general(table, cross, (((1,), (1,)), ((), ())), preferred_element_type=jnp.float32)


def kernel(
    dims, records_hbm, visits_hbm, forward_hbm, inverse_hbm, out,
    visits, records, forward, inverse, whitened, held, held_visits, own_select, held_select, terms,
    early_out, late_out, back_out, early_in, late_in, back_in,
    load_sem, table_sem, block_send, block_recv, visit_send, visit_recv,
    early_send, early_recv, late_send, late_recv, back_send, back_recv,
):
    reach, days, segs, blocks, sets, width, picks, scale = dims
    groups = days * segs
    share = LAGS // groups
    cols = picks * width
    chan = lax.axis_index("chan")
    group = lax.axis_index("day") * segs + lax.axis_index("seg")

    def at(offset, step):
        other = lax.rem(group + step, groups)
        return {"chan": lax.rem(chan + offset + blocks, blocks), "day": other // segs, "seg": lax.rem(other, segs)}

    load_records = pltpu.make_async_copy(records_hbm, records, load_sem.at[0])
    load_inverse = pltpu.make_async_copy(inverse_hbm, inverse, load_sem.at[1])
    load_visits = pltpu.make_async_copy(visits_hbm, visits, load_sem.at[2])
    load_table = [
        pltpu.make_async_copy(forward_hbm.at[c], forward.at[c], table_sem.at[c]) for c in range(CHUNKS)
    ]
    load_visits.start()
    load_records.start()
    load_table[0].start()

    barrier = pltpu.get_barrier_semaphore()
    partners = [(o, k) for o in range(-reach, reach + 1) for k in range(groups) if (o, k) != (0, 0)]
    for o, k in partners:
        pl.semaphore_signal(barrier, inc=1, device_id=at(o, k), device_id_type=MESH)
    for c in range(1, CHUNKS):
        load_table[c].start()
    load_inverse.start()

    load_visits.wait()
    for o in range(reach + 1):
        own_select[o] = selector(visits[reach + o], sets, width)

    send_visits, send_blocks = [], []
    load_records.wait()
    for c in range(CHUNKS):
        load_table[c].wait()
        spectra = jnp.dot(records[...], forward[c], preferred_element_type=jnp.float32)
        whitened[c] = whiten(spectra)
        if c == 0:
            pl.semaphore_wait(barrier, len(partners))
            for o in range(1, reach + 1):
                copy = pltpu.make_async_remote_copy(
                    visits.at[reach - o], held_visits.at[o - 1], visit_send.at[o - 1], visit_recv.at[o - 1],
                    device_id=at(o, 0), device_id_type=MESH,
                )
                copy.start()
                send_visits.append(copy)
        for o in range(1, reach + 1):
            copy = pltpu.make_async_remote_copy(
                whitened.at[c], held.at[o - 1, c], block_send.at[o - 1, c], block_recv.at[o - 1, c],
                device_id=at(o, 0), device_id_type=MESH,
            )
            copy.start()
            send_blocks.append(copy)
        if c == 0:
            load_inverse.wait()
        mine = whitened[c]
        cross = cross_spectrum(mine, mine, own_select[0], sets, width)
        part = lag_terms(inverse[c], cross).reshape(groups, share, cols)
        terms[reach] = part if c == 0 else terms[reach] + part

    early_out[...] = terms[reach].astype(jnp.bfloat16)
    send_results = []

    def send_result(source, target, send, recv, offset, step):
        other = lax.rem(group + step, groups)
        copy = pltpu.make_async_remote_copy(
            source.at[other], target.at[step], send.at[step], recv.at[step],
            device_id=at(offset, step), device_id_type=MESH,
        )
        copy.start()
        send_results.append(copy)

    for k in range(1, groups):
        send_result(early_out, early_in, early_send, early_recv, 0, k)

    for o in range(1, reach + 1):
        send_visits[o - 1].wait_recv()
        held_select[o - 1] = selector(held_visits[o - 1], sets, width)

    for c in range(CHUNKS):
        for o in range(1, reach + 1):
            send_blocks[c * reach + o - 1].wait_recv()
            mine, theirs = whitened[c], held[o - 1, c]
            down = cross_spectrum(mine, theirs, own_select[o], sets, width)
            up = cross_spectrum(theirs, mine, held_select[o - 1], sets, width)
            part = lag_terms(inverse[c], jnp.concatenate([down, up], 0))
            for place, piece in ((reach + o, part[:, :cols]), (reach - o, part[:, cols:])):
                piece = piece.reshape(groups, share, cols)
                terms[place] = piece if c == 0 else terms[place] + piece

    for o in range(1, reach + 1):
        back_out[o - 1] = terms[reach - o].astype(jnp.bfloat16)
        for k in range(groups):
            send_result(back_out.at[o - 1], back_in.at[o - 1], back_send.at[o - 1], back_recv.at[o - 1], -o, k)
        late_out[:, :, (o - 1) * cols : o * cols] = terms[reach + o].astype(jnp.bfloat16)
    for k in range(1, groups):
        send_result(late_out, late_in, late_send, late_recv, 0, k)

    for copy in send_results:
        copy.wait_recv()
    total = terms[reach, group]
    for k in range(1, groups):
        total += early_in[k].astype(jnp.float32)
    out[:, reach * cols : (reach + 1) * cols] = (total * scale).astype(jnp.bfloat16)
    for o in range(1, reach + 1):
        total = back_in[o - 1, 0].astype(jnp.float32)
        for k in range(1, groups):
            total += back_in[o - 1, k].astype(jnp.float32)
        out[:, (reach - o) * cols : (reach - o + 1) * cols] = (total * scale).astype(jnp.bfloat16)
        total = terms[reach + o, group]
        for k in range(1, groups):
            total += late_in[k, :, (o - 1) * cols : o * cols].astype(jnp.float32)
        out[:, (reach + o) * cols : (reach + o + 1) * cols] = (total * scale).astype(jnp.bfloat16)
    for copy in send_visits + send_blocks + send_results:
        copy.wait_send()


def local(records, visits):
    day_local, seg_local, width, samples = records.shape
    visit_count, picks, _ = visits.shape
    days, segs, blocks = lax.axis_size("day"), lax.axis_size("seg"), lax.axis_size("chan")
    reach = blocks // 4
    groups = days * segs
    share = LAGS // groups
    sets = day_local * seg_local
    rows = sets * width
    cols = picks * width
    scale = 1.0 / math.sqrt(FREQS * day_local * days * SEGS)
    bf16, f32 = jnp.bfloat16, jnp.float32
    hbm = pl.BlockSpec(memory_space=pltpu.HBM)
    vmem = pl.BlockSpec(memory_space=pltpu.VMEM)
    dma = pltpu.SemaphoreType.DMA
    flops = 2 * rows * samples * 2 * FREQS + 2 * LAGS * 2 * FREQS * visit_count * cols
    result = pl.pallas_call(
        functools.partial(kernel, (reach, days, segs, blocks, sets, width, picks, scale)),
        out_shape=jax.ShapeDtypeStruct((share, visit_count * cols), bf16),
        in_specs=[hbm, hbm, hbm, hbm],
        out_specs=vmem,
        scratch_shapes=[
            pltpu.VMEM((visit_count, picks, width), jnp.int32),
            pltpu.VMEM((rows, samples), bf16),
            pltpu.VMEM((CHUNKS, samples, 2 * WIDE), bf16),
            pltpu.VMEM((CHUNKS, LAGS, 2 * WIDE), bf16),
            pltpu.VMEM((CHUNKS, rows, 2 * WIDE), bf16),
            pltpu.VMEM((reach, CHUNKS, rows, 2 * WIDE), bf16),
            pltpu.VMEM((reach, picks, width), jnp.int32),
            pltpu.VMEM((reach + 1, sets * cols, rows), bf16),
            pltpu.VMEM((reach, sets * cols, rows), bf16),
            pltpu.VMEM((visit_count, groups, share, cols), f32),
            pltpu.VMEM((groups, share, cols), bf16),
            pltpu.VMEM((groups, share, reach * cols), bf16),
            pltpu.VMEM((reach, groups, share, cols), bf16),
            pltpu.VMEM((groups, share, cols), bf16),
            pltpu.VMEM((groups, share, reach * cols), bf16),
            pltpu.VMEM((reach, groups, share, cols), bf16),
            dma((3,)), dma((CHUNKS,)), dma((reach, CHUNKS)), dma((reach, CHUNKS)), dma((reach,)), dma((reach,)),
            dma((groups,)), dma((groups,)), dma((groups,)), dma((groups,)),
            dma((reach, groups)), dma((reach, groups)),
        ],
        compiler_params=pltpu.CompilerParams(
            collective_id=0, has_side_effects=True, vmem_limit_bytes=56 * 1024 * 1024
        ),
        cost_estimate=pl.CostEstimate(flops=flops, bytes_accessed=8 * 1024 * 1024, transcendentals=0),
        name="correlate",
    )(records.reshape(rows, samples), visits, forward_chunks(samples), inverse_chunks(samples))
    return result.reshape(share, visit_count, picks, width)


def solution(mesh):
    in_specs = (P("day", "seg", ("grp", "chan"), None), P(None, None, ("grp", "chan")))
    out_specs = P(("day", "seg"), None, None, ("grp", "chan"))
    return jax.shard_map(local, mesh=mesh, in_specs=in_specs, out_specs=out_specs, check_vma=False)
```

```python
import functools
import math

import jax
import jax.numpy as jnp
import ml_dtypes
import numpy as np
from jax import lax
from jax.experimental import pallas as pl
from jax.experimental.pallas import tpu as pltpu
from jax.sharding import PartitionSpec as P

FREQS = 512
BAND = 64
LAGS = 256
SEGS = 4
WIDE = 128
CHUNKS = FREQS // WIDE
MESH = pl.DeviceIdType.MESH


def forward_chunks(samples):
    index = np.arange(samples)[:, None] * np.arange(FREQS)[None, :] % samples
    turns = index * (2.0 * math.pi / samples)
    table = np.stack([np.cos(turns), -np.sin(turns)], 1).reshape(samples, 2, CHUNKS, WIDE)
    return table.transpose(2, 0, 1, 3).reshape(CHUNKS, samples, 2 * WIDE).astype(ml_dtypes.bfloat16)


def inverse_chunks(samples):
    index = (np.arange(LAGS) - LAGS // 2)[:, None] * np.arange(FREQS)[None, :] % samples
    turns = index * (2.0 * math.pi / samples)
    table = np.stack([np.cos(turns), -np.sin(turns)], 1).reshape(LAGS, 2, CHUNKS, WIDE)
    return table.transpose(2, 0, 1, 3).reshape(CHUNKS, LAGS, 2 * WIDE).astype(ml_dtypes.bfloat16)


def selector(picks, sets, width):
    pick_count = picks.shape[0]
    across = lax.broadcasted_iota(jnp.int32, (width, width), 1)
    down = lax.broadcasted_iota(jnp.int32, (width, width), 0)
    columns = []
    for p in range(pick_count):
        row = picks[p : p + 1, :].astype(jnp.float32)
        diagonal = jnp.where(across == down, jnp.broadcast_to(row, (width, width)), 0.0)
        columns.append(jnp.sum(diagonal, axis=1, keepdims=True))
    column = jnp.concatenate(columns, 0)
    place = lax.broadcasted_iota(jnp.int32, (pick_count * width, sets * width), 1).astype(jnp.float32)
    rows = [jnp.where(place == column + float(s * width), 1.0, 0.0) for s in range(sets)]
    return jnp.concatenate(rows, 0).astype(jnp.bfloat16)


def whiten(spectra):
    real_part = spectra[:, :WIDE]
    imag_part = spectra[:, WIDE:]
    square = real_part * real_part + imag_part * imag_part
    high = square.astype(jnp.bfloat16)
    low = (square - high.astype(jnp.float32)).astype(jnp.bfloat16)
    down = lax.broadcasted_iota(jnp.int32, (WIDE, WIDE), 0) // BAND
    across = lax.broadcasted_iota(jnp.int32, (WIDE, WIDE), 1) // BAND
    mean = jnp.where(down == across, 0.5 / BAND, 0.0).astype(jnp.bfloat16)
    power = jnp.dot(high, mean, preferred_element_type=jnp.float32)
    power += jnp.dot(low, mean, preferred_element_type=jnp.float32)
    factor = lax.rsqrt(power + 1e-06)
    return jnp.concatenate([real_part * factor, imag_part * factor], 1).astype(jnp.bfloat16)


def cross_sums(own, other, select, width):
    sets = own.shape[0] // width
    picked = jnp.dot(select, other, preferred_element_type=jnp.float32)
    rows = picked.shape[0] // sets
    real_sum = jnp.zeros((rows, WIDE), jnp.float32)
    imag_sum = jnp.zeros((rows, WIDE), jnp.float32)
    for s in range(sets):
        mine = own[s * width : (s + 1) * width].astype(jnp.float32)
        mine = jnp.concatenate([mine] * (rows // width), 0)
        theirs = picked[s * rows : (s + 1) * rows]
        mine_re, mine_im = mine[:, :WIDE], mine[:, WIDE:]
        their_re, their_im = theirs[:, :WIDE], theirs[:, WIDE:]
        real_sum += mine_re * their_re + mine_im * their_im
        imag_sum += mine_re * their_im - mine_im * their_re
    return jnp.concatenate([real_sum, imag_sum], 1)


def lag_terms(table, cross):
    return lax.dot_general(table, cross, (((1,), (1,)), ((), ())), preferred_element_type=jnp.float32)


def kernel(
    dims, records_hbm, visits_hbm, forward_hbm, inverse_hbm, out,
    visits, records, forward, inverse, whitened, held, held_visits, own_select, held_select, terms,
    early_out, late_out, back_out, early_in, late_in, back_in,
    load_sem, table_sem, block_send, block_recv, visit_send, visit_recv,
    early_send, early_recv, late_send, late_recv, back_send, back_recv,
):
    reach, days, segs, blocks, sets, width, picks, scale = dims
    groups = days * segs
    share = LAGS // groups
    cols = picks * width
    chan = lax.axis_index("chan")
    group = lax.axis_index("day") * segs + lax.axis_index("seg")

    def at(offset, step):
        other = lax.rem(group + step, groups)
        return {"chan": lax.rem(chan + offset + blocks, blocks), "day": other // segs, "seg": lax.rem(other, segs)}

    load_records = pltpu.make_async_copy(records_hbm, records, load_sem.at[0])
    load_inverse = pltpu.make_async_copy(inverse_hbm, inverse, load_sem.at[1])
    load_visits = pltpu.make_async_copy(visits_hbm, visits, load_sem.at[2])
    load_table = [
        pltpu.make_async_copy(forward_hbm.at[c], forward.at[c], table_sem.at[c]) for c in range(CHUNKS)
    ]
    load_visits.start()
    load_records.start()
    load_table[0].start()

    barrier = pltpu.get_barrier_semaphore()
    partners = [(o, k) for o in range(-reach, reach + 1) for k in range(groups) if (o, k) != (0, 0)]
    for o, k in partners:
        pl.semaphore_signal(barrier, inc=1, device_id=at(o, k), device_id_type=MESH)
    for c in range(1, CHUNKS):
        load_table[c].start()
    load_inverse.start()

    halves = [(0, sets // 2), (sets // 2, sets // 2)] if sets % 2 == 0 else [(0, sets)]
    pieces = [halves if c in (0, CHUNKS - 1) else [(0, sets)] for c in range(CHUNKS)]

    def block_rows(piece):
        return pl.ds(piece[0] * width, piece[1] * width)

    send_visits, send_blocks = [], {}
    load_records.wait()
    for c in range(CHUNKS):
        load_table[c].wait()
        for i, piece in enumerate(pieces[c]):
            spectra = jnp.dot(records[block_rows(piece)], forward[c], preferred_element_type=jnp.float32)
            whitened[c, block_rows(piece)] = whiten(spectra)
            if c == 0 and i == 0:
                pl.semaphore_wait(barrier, len(partners))
            for o in range(1, reach + 1):
                copy = pltpu.make_async_remote_copy(
                    whitened.at[c, block_rows(piece)], held.at[o - 1, c, block_rows(piece)],
                    block_send.at[o - 1, c, i], block_recv.at[o - 1, c, i],
                    device_id=at(o, 0), device_id_type=MESH,
                )
                copy.start()
                send_blocks[c, o, i] = copy
        if c == 0:
            load_visits.wait()
            for o in range(1, reach + 1):
                copy = pltpu.make_async_remote_copy(
                    visits.at[reach - o], held_visits.at[o - 1], visit_send.at[o - 1], visit_recv.at[o - 1],
                    device_id=at(o, 0), device_id_type=MESH,
                )
                copy.start()
                send_visits.append(copy)
            for o in range(reach + 1):
                own_select[o] = selector(visits[reach + o], sets, width)
            load_inverse.wait()
        mine = whitened[c]
        cross = cross_sums(mine, mine, own_select[0], width).astype(jnp.bfloat16)
        part = lag_terms(inverse[c], cross).reshape(groups, share, cols)
        terms[reach] = part if c == 0 else terms[reach] + part

    send_results = []

    def send_result(source, target, send, recv, offset, step):
        other = lax.rem(group + step, groups)
        copy = pltpu.make_async_remote_copy(
            source.at[other], target.at[step], send.at[step], recv.at[step],
            device_id=at(offset, step), device_id_type=MESH,
        )
        copy.start()
        send_results.append(copy)
        return copy

    def finish(place, total, copies, target):
        for copy, k in copies:
            copy.wait_recv()
            total += target[k].astype(jnp.float32)
        out[:, place * cols : (place + 1) * cols] = (total * scale).astype(jnp.bfloat16)

    early_out[...] = terms[reach].astype(jnp.bfloat16)
    early = [(send_result(early_out, early_in, early_send, early_recv, 0, k), k) for k in range(1, groups)]

    for o in range(1, reach + 1):
        send_visits[o - 1].wait_recv()
        held_select[o - 1] = selector(held_visits[o - 1], sets, width)

    back, late = {}, {}
    for c in range(CHUNKS):
        if c == CHUNKS - 1:
            finish(reach, terms[reach, group], early, early_in)
        for o in range(1, reach + 1):
            up, down = 0.0, 0.0
            for i, piece in enumerate(pieces[c]):
                send_blocks[c, o, i].wait_recv()
                mine, theirs = whitened[c, block_rows(piece)], held[o - 1, c, block_rows(piece)]
                part = (slice(0, piece[1] * cols), slice(0, piece[1] * width))
                up += cross_sums(theirs, mine, held_select[o - 1][part], width)
                if c == CHUNKS - 1 and i == len(pieces[c]) - 1:
                    last = lag_terms(inverse[c], up.astype(jnp.bfloat16)).reshape(groups, share, cols)
                    back_out[o - 1] = (terms[reach - o] + last).astype(jnp.bfloat16)
                    refs = [ref.at[o - 1] for ref in (back_out, back_in, back_send, back_recv)]
                    back[o] = [(send_result(*refs, -o, k), k) for k in range(groups)]
                down += cross_sums(mine, theirs, own_select[o][part], width)
            if c < CHUNKS - 1:
                both = jnp.concatenate([down, up], 0).astype(jnp.bfloat16)
                both = lag_terms(inverse[c], both)
                for place, piece in ((reach + o, both[:, :cols]), (reach - o, both[:, cols:])):
                    piece = piece.reshape(groups, share, cols)
                    terms[place] = piece if c == 0 else terms[place] + piece
            else:
                last = lag_terms(inverse[c], down.astype(jnp.bfloat16)).reshape(groups, share, cols)
                last += terms[reach + o]
                terms[reach + o] = last
                late_out[o - 1] = last.astype(jnp.bfloat16)
                refs = [ref.at[o - 1] for ref in (late_out, late_in, late_send, late_recv)]
                late[o] = [(send_result(*refs, 0, k), k) for k in range(1, groups)]

    for o in range(1, reach + 1):
        finish(reach - o, 0.0, back[o], back_in.at[o - 1])
        finish(reach + o, terms[reach + o, group], late[o], late_in.at[o - 1])
    for copy in send_visits + list(send_blocks.values()) + send_results:
        copy.wait_send()


def local(records, visits):
    day_local, seg_local, width, samples = records.shape
    visit_count, picks, _ = visits.shape
    days, segs, blocks = lax.axis_size("day"), lax.axis_size("seg"), lax.axis_size("chan")
    reach = blocks // 4
    groups = days * segs
    share = LAGS // groups
    sets = day_local * seg_local
    rows = sets * width
    cols = picks * width
    scale = 1.0 / math.sqrt(FREQS * day_local * days * SEGS)
    bf16, f32 = jnp.bfloat16, jnp.float32
    hbm = pl.BlockSpec(memory_space=pltpu.HBM)
    vmem = pl.BlockSpec(memory_space=pltpu.VMEM)
    dma = pltpu.SemaphoreType.DMA
    flops = 2 * rows * samples * 2 * FREQS + 2 * LAGS * 2 * FREQS * visit_count * cols
    result = pl.pallas_call(
        functools.partial(kernel, (reach, days, segs, blocks, sets, width, picks, scale)),
        out_shape=jax.ShapeDtypeStruct((share, visit_count * cols), bf16),
        in_specs=[hbm, hbm, hbm, hbm],
        out_specs=vmem,
        scratch_shapes=[
            pltpu.VMEM((visit_count, picks, width), jnp.int32),
            pltpu.VMEM((rows, samples), bf16),
            pltpu.VMEM((CHUNKS, samples, 2 * WIDE), bf16),
            pltpu.VMEM((CHUNKS, LAGS, 2 * WIDE), bf16),
            pltpu.VMEM((CHUNKS, rows, 2 * WIDE), bf16),
            pltpu.VMEM((reach, CHUNKS, rows, 2 * WIDE), bf16),
            pltpu.VMEM((reach, picks, width), jnp.int32),
            pltpu.VMEM((reach + 1, sets * cols, rows), bf16),
            pltpu.VMEM((reach, sets * cols, rows), bf16),
            pltpu.VMEM((visit_count, groups, share, cols), f32),
            pltpu.VMEM((groups, share, cols), bf16),
            pltpu.VMEM((reach, groups, share, cols), bf16),
            pltpu.VMEM((reach, groups, share, cols), bf16),
            pltpu.VMEM((groups, share, cols), bf16),
            pltpu.VMEM((reach, groups, share, cols), bf16),
            pltpu.VMEM((reach, groups, share, cols), bf16),
            dma((3,)), dma((CHUNKS,)), dma((reach, CHUNKS, 2)), dma((reach, CHUNKS, 2)), dma((reach,)), dma((reach,)),
            dma((groups,)), dma((groups,)), dma((reach, groups)), dma((reach, groups)),
            dma((reach, groups)), dma((reach, groups)),
        ],
        compiler_params=pltpu.CompilerParams(
            collective_id=0, has_side_effects=True, vmem_limit_bytes=32 * 1024 * 1024
        ),
        cost_estimate=pl.CostEstimate(flops=flops, bytes_accessed=8 * 1024 * 1024, transcendentals=0),
        name="correlate",
    )(records.reshape(rows, samples), visits, forward_chunks(samples), inverse_chunks(samples))
    return result.reshape(share, visit_count, picks, width)


def solution(mesh):
    in_specs = (P("day", "seg", ("grp", "chan"), None), P(None, None, ("grp", "chan")))
    out_specs = P(("day", "seg"), None, None, ("grp", "chan"))
    return jax.shard_map(local, mesh=mesh, in_specs=in_specs, out_specs=out_specs, check_vma=False)
```

```python
import functools
import math

import jax
import jax.numpy as jnp
import ml_dtypes
import numpy as np
from jax import lax
from jax.experimental import pallas as pl
from jax.experimental.pallas import tpu as pltpu
from jax.sharding import PartitionSpec as P

FREQS = 512
BAND = 64
LAGS = 256
SEGS = 4
WIDE = 128
CHUNKS = FREQS // WIDE
MESH = pl.DeviceIdType.MESH


def forward_chunks(samples):
    index = np.arange(samples)[:, None] * np.arange(FREQS)[None, :] % samples
    turns = index * (2.0 * math.pi / samples)
    table = np.stack([np.cos(turns), -np.sin(turns)], 1).reshape(samples, 2, CHUNKS, WIDE)
    return table.transpose(2, 0, 1, 3).reshape(CHUNKS, samples, 2 * WIDE).astype(ml_dtypes.bfloat16)


def inverse_chunks(samples):
    index = (np.arange(LAGS) - LAGS // 2)[:, None] * np.arange(FREQS)[None, :] % samples
    turns = index * (2.0 * math.pi / samples)
    table = np.stack([np.cos(turns), -np.sin(turns)], 1).reshape(LAGS, 2, CHUNKS, WIDE)
    return table.transpose(2, 0, 1, 3).reshape(CHUNKS, LAGS, 2 * WIDE).astype(ml_dtypes.bfloat16)


def selector(picks, sets, width):
    pick_count = picks.shape[0]
    across = lax.broadcasted_iota(jnp.int32, (width, width), 1)
    down = lax.broadcasted_iota(jnp.int32, (width, width), 0)
    columns = []
    for p in range(pick_count):
        row = picks[p : p + 1, :].astype(jnp.float32)
        diagonal = jnp.where(across == down, jnp.broadcast_to(row, (width, width)), 0.0)
        columns.append(jnp.sum(diagonal, axis=1, keepdims=True))
    column = jnp.concatenate(columns, 0)
    place = lax.broadcasted_iota(jnp.int32, (pick_count * width, sets * width), 1).astype(jnp.float32)
    rows = [jnp.where(place == column + float(s * width), 1.0, 0.0) for s in range(sets)]
    return jnp.concatenate(rows, 0).astype(jnp.bfloat16)


def whiten(spectra):
    real_part = spectra[:, :WIDE]
    imag_part = spectra[:, WIDE:]
    square = real_part * real_part + imag_part * imag_part
    high = square.astype(jnp.bfloat16)
    low = (square - high.astype(jnp.float32)).astype(jnp.bfloat16)
    down = lax.broadcasted_iota(jnp.int32, (WIDE, WIDE), 0) // BAND
    across = lax.broadcasted_iota(jnp.int32, (WIDE, WIDE), 1) // BAND
    mean = jnp.where(down == across, 0.5 / BAND, 0.0).astype(jnp.bfloat16)
    power = jnp.dot(high, mean, preferred_element_type=jnp.float32)
    power += jnp.dot(low, mean, preferred_element_type=jnp.float32)
    factor = lax.rsqrt(power + 1e-06)
    return jnp.concatenate([real_part * factor, imag_part * factor], 1).astype(jnp.bfloat16)


def cross_sums(own, other, select, width):
    sets = own.shape[0] // width
    picked = jnp.dot(select, other, preferred_element_type=jnp.float32)
    rows = picked.shape[0] // sets
    real_sum = jnp.zeros((rows, WIDE), jnp.float32)
    imag_sum = jnp.zeros((rows, WIDE), jnp.float32)
    for s in range(sets):
        mine = own[s * width : (s + 1) * width].astype(jnp.float32)
        mine = jnp.concatenate([mine] * (rows // width), 0)
        theirs = picked[s * rows : (s + 1) * rows]
        mine_re, mine_im = mine[:, :WIDE], mine[:, WIDE:]
        their_re, their_im = theirs[:, :WIDE], theirs[:, WIDE:]
        real_sum += mine_re * their_re + mine_im * their_im
        imag_sum += mine_re * their_im - mine_im * their_re
    return jnp.concatenate([real_sum, imag_sum], 1)


def lag_terms(table, cross):
    return lax.dot_general(table, cross, (((1,), (1,)), ((), ())), preferred_element_type=jnp.float32)


def kernel(
    dims, records_hbm, visits_hbm, forward_hbm, inverse_hbm, out,
    visits, records, forward, inverse, whitened, held, held_visits, own_select, held_select, terms,
    early_out, late_out, back_out, early_in, late_in, back_in,
    load_sem, table_sem, block_send, block_recv, visit_send, visit_recv,
    early_send, early_recv, late_send, late_recv, back_send, back_recv,
):
    reach, days, segs, blocks, sets, width, picks, scale = dims
    groups = days * segs
    share = LAGS // groups
    cols = picks * width
    chan = lax.axis_index("chan")
    group = lax.axis_index("day") * segs + lax.axis_index("seg")

    def at(offset, step):
        other = lax.rem(group + step, groups)
        return {"chan": lax.rem(chan + offset + blocks, blocks), "day": other // segs, "seg": lax.rem(other, segs)}

    load_records = pltpu.make_async_copy(records_hbm, records, load_sem.at[0])
    load_inverse = pltpu.make_async_copy(inverse_hbm, inverse, load_sem.at[1])
    load_visits = pltpu.make_async_copy(visits_hbm, visits, load_sem.at[2])
    load_table = [
        pltpu.make_async_copy(forward_hbm.at[c], forward.at[c], table_sem.at[c]) for c in range(CHUNKS)
    ]
    load_visits.start()
    load_records.start()
    load_table[0].start()

    barrier = pltpu.get_barrier_semaphore()
    partners = [(o, k) for o in range(-reach, reach + 1) for k in range(groups) if (o, k) != (0, 0)]
    for o, k in partners:
        pl.semaphore_signal(barrier, inc=1, device_id=at(o, k), device_id_type=MESH)
    for c in range(1, CHUNKS):
        load_table[c].start()
    load_inverse.start()

    halves = [(0, sets // 2), (sets // 2, sets // 2)] if sets % 2 == 0 else [(0, sets)]
    pieces = [halves if c in (0, CHUNKS - 1) else [(0, sets)] for c in range(CHUNKS)]

    def block_rows(piece):
        return pl.ds(piece[0] * width, piece[1] * width)

    send_visits, send_blocks = [], {}
    load_records.wait()
    for c in range(CHUNKS):
        load_table[c].wait()
        for i, piece in enumerate(pieces[c]):
            spectra = jnp.dot(records[block_rows(piece)], forward[c], preferred_element_type=jnp.float32)
            whitened[c, block_rows(piece)] = whiten(spectra)
            if c == 0 and i == 0:
                pl.semaphore_wait(barrier, len(partners))
            for o in range(1, reach + 1):
                copy = pltpu.make_async_remote_copy(
                    whitened.at[c, block_rows(piece)], held.at[o - 1, c, block_rows(piece)],
                    block_send.at[o - 1, c, i], block_recv.at[o - 1, c, i],
                    device_id=at(o, 0), device_id_type=MESH,
                )
                copy.start()
                send_blocks[c, o, i] = copy
        if c == 0:
            load_visits.wait()
            for o in range(1, reach + 1):
                copy = pltpu.make_async_remote_copy(
                    visits.at[reach - o], held_visits.at[o - 1], visit_send.at[o - 1], visit_recv.at[o - 1],
                    device_id=at(o, 0), device_id_type=MESH,
                )
                copy.start()
                send_visits.append(copy)
            for o in range(reach + 1):
                own_select[o] = selector(visits[reach + o], sets, width)
            load_inverse.wait()
        mine = whitened[c]
        cross = cross_sums(mine, mine, own_select[0], width).astype(jnp.bfloat16)
        part = lag_terms(inverse[c], cross).reshape(groups, share, cols)
        terms[reach] = part if c == 0 else terms[reach] + part

    send_results = []

    def send_result(source, target, send, recv, offset, step):
        other = lax.rem(group + step, groups)
        copy = pltpu.make_async_remote_copy(
            source.at[other], target.at[step], send.at[step], recv.at[step],
            device_id=at(offset, step), device_id_type=MESH,
        )
        copy.start()
        send_results.append(copy)
        return copy

    def finish(place, total, copies, target):
        for copy, k in copies:
            copy.wait_recv()
            total += target[k].astype(jnp.float32)
        out[:, place * cols : (place + 1) * cols] = (total * scale).astype(jnp.bfloat16)

    early_out[...] = terms[reach].astype(jnp.bfloat16)
    early = [(send_result(early_out, early_in, early_send, early_recv, 0, k), k) for k in range(1, groups)]

    for o in range(1, reach + 1):
        send_visits[o - 1].wait_recv()
        held_select[o - 1] = selector(held_visits[o - 1], sets, width)

    back, late = {}, {}
    for c in range(CHUNKS):
        if c == CHUNKS - 1:
            finish(reach, terms[reach, group], early, early_in)
        for o in range(1, reach + 1):
            up, down = 0.0, 0.0
            for i, piece in enumerate(pieces[c]):
                send_blocks[c, o, i].wait_recv()
                mine, theirs = whitened[c, block_rows(piece)], held[o - 1, c, block_rows(piece)]
                part = (slice(0, piece[1] * cols), slice(0, piece[1] * width))
                up += cross_sums(theirs, mine, held_select[o - 1][part], width)
                if c == CHUNKS - 1 and i == len(pieces[c]) - 1:
                    last = lag_terms(inverse[c], up.astype(jnp.bfloat16)).reshape(groups, share, cols)
                    back_out[o - 1] = (terms[reach - o] + last).astype(jnp.bfloat16)
                    refs = [ref.at[o - 1] for ref in (back_out, back_in, back_send, back_recv)]
                    back[o] = [(send_result(*refs, -o, k), k) for k in range(groups)]
                down += cross_sums(mine, theirs, own_select[o][part], width)
            if c < CHUNKS - 1:
                both = jnp.concatenate([down, up], 0).astype(jnp.bfloat16)
                both = lag_terms(inverse[c], both)
                for place, piece in ((reach + o, both[:, :cols]), (reach - o, both[:, cols:])):
                    piece = piece.reshape(groups, share, cols)
                    terms[place] = piece if c == 0 else terms[place] + piece
            else:
                last = lag_terms(inverse[c], down.astype(jnp.bfloat16)).reshape(groups, share, cols)
                last += terms[reach + o]
                terms[reach + o] = last
                late_out[o - 1] = last.astype(jnp.bfloat16)
                refs = [ref.at[o - 1] for ref in (late_out, late_in, late_send, late_recv)]
                late[o] = [(send_result(*refs, 0, k), k) for k in range(1, groups)]

    for o in range(1, reach + 1):
        finish(reach - o, 0.0, back[o], back_in.at[o - 1])
        finish(reach + o, terms[reach + o, group], late[o], late_in.at[o - 1])
    for copy in send_visits + list(send_blocks.values()) + send_results:
        copy.wait_send()


def local(records, visits):
    day_local, seg_local, width, samples = records.shape
    visit_count, picks, _ = visits.shape
    days, segs, blocks = lax.axis_size("day"), lax.axis_size("seg"), lax.axis_size("chan")
    reach = blocks // 4
    groups = days * segs
    share = LAGS // groups
    sets = day_local * seg_local
    rows = sets * width
    cols = picks * width
    scale = 1.0 / math.sqrt(FREQS * day_local * days * SEGS)
    bf16, f32 = jnp.bfloat16, jnp.float32
    hbm = pl.BlockSpec(memory_space=pltpu.HBM)
    vmem = pl.BlockSpec(memory_space=pltpu.VMEM)
    dma = pltpu.SemaphoreType.DMA
    flops = 2 * rows * samples * 2 * FREQS + 2 * LAGS * 2 * FREQS * visit_count * cols
    operands = (records.reshape(rows, samples), visits, forward_chunks(samples), inverse_chunks(samples))
    result = pl.pallas_call(
        functools.partial(kernel, (reach, days, segs, blocks, sets, width, picks, scale)),
        out_shape=jax.ShapeDtypeStruct((share, visit_count * cols), bf16),
        in_specs=[hbm, hbm, hbm, hbm],
        out_specs=vmem,
        scratch_shapes=[
            pltpu.VMEM((visit_count, picks, width), jnp.int32),
            pltpu.VMEM((rows, samples), bf16),
            pltpu.VMEM((CHUNKS, samples, 2 * WIDE), bf16),
            pltpu.VMEM((CHUNKS, LAGS, 2 * WIDE), bf16),
            pltpu.VMEM((CHUNKS, rows, 2 * WIDE), bf16),
            pltpu.VMEM((reach, CHUNKS, rows, 2 * WIDE), bf16),
            pltpu.VMEM((reach, picks, width), jnp.int32),
            pltpu.VMEM((reach + 1, sets * cols, rows), bf16),
            pltpu.VMEM((reach, sets * cols, rows), bf16),
            pltpu.VMEM((visit_count, groups, share, cols), f32),
            pltpu.VMEM((groups, share, cols), bf16),
            pltpu.VMEM((reach, groups, share, cols), bf16),
            pltpu.VMEM((reach, groups, share, cols), bf16),
            pltpu.VMEM((groups, share, cols), bf16),
            pltpu.VMEM((reach, groups, share, cols), bf16),
            pltpu.VMEM((reach, groups, share, cols), bf16),
            dma((3,)), dma((CHUNKS,)), dma((reach, CHUNKS, 2)), dma((reach, CHUNKS, 2)), dma((reach,)), dma((reach,)),
            dma((groups,)), dma((groups,)), dma((reach, groups)), dma((reach, groups)),
            dma((reach, groups)), dma((reach, groups)),
        ],
        compiler_params=pltpu.CompilerParams(
            collective_id=0, has_side_effects=True, vmem_limit_bytes=32 * 1024 * 1024
        ),
        cost_estimate=pl.CostEstimate(flops=flops, bytes_accessed=8 * 1024 * 1024, transcendentals=0),
        name="correlate",
    )(*(pltpu.with_memory_space_constraint(jnp.asarray(x), pltpu.HBM) for x in operands))
    return result.reshape(share, visit_count, picks, width)


def solution(mesh):
    in_specs = (P("day", "seg", ("grp", "chan"), None), P(None, None, ("grp", "chan")))
    out_specs = P(("day", "seg"), None, None, ("grp", "chan"))
    return jax.shard_map(local, mesh=mesh, in_specs=in_specs, out_specs=out_specs, check_vma=False)
```

```python
import functools
import math

import jax
import jax.numpy as jnp
import ml_dtypes
import numpy as np
from jax import lax
from jax.experimental import pallas as pl
from jax.experimental.pallas import tpu as pltpu
from jax.sharding import PartitionSpec as P

FREQS = 512
BAND = 64
LAGS = 256
SEGS = 4
WIDE = 128
CHUNKS = FREQS // WIDE
MESH = pl.DeviceIdType.MESH


def forward_chunks(samples):
    index = np.arange(samples // 2)[:, None] * np.arange(FREQS)[None, :] % samples
    turns = index * (2.0 * math.pi / samples)
    table = np.stack([np.cos(turns), -np.sin(turns)], 1).reshape(samples // 2, 2, CHUNKS, WIDE)
    return table.transpose(2, 0, 1, 3).reshape(CHUNKS, samples // 2, 2 * WIDE).astype(ml_dtypes.bfloat16)


def inverse_chunks(samples):
    index = (np.arange(LAGS) - LAGS // 2)[:, None] * np.arange(FREQS)[None, :] % samples
    turns = index * (2.0 * math.pi / samples)
    table = np.stack([np.cos(turns), -np.sin(turns)], 1).reshape(LAGS, 2, CHUNKS, WIDE)
    return table.transpose(2, 0, 1, 3).reshape(CHUNKS, LAGS, 2 * WIDE).astype(ml_dtypes.bfloat16)


def selector(picks, sets, width):
    pick_count = picks.shape[0]
    across = lax.broadcasted_iota(jnp.int32, (width, width), 1)
    down = lax.broadcasted_iota(jnp.int32, (width, width), 0)
    columns = []
    for p in range(pick_count):
        row = picks[p : p + 1, :].astype(jnp.float32)
        diagonal = jnp.where(across == down, jnp.broadcast_to(row, (width, width)), 0.0)
        columns.append(jnp.sum(diagonal, axis=1, keepdims=True))
    column = jnp.concatenate(columns, 0)
    place = lax.broadcasted_iota(jnp.int32, (pick_count * width, sets * width), 1).astype(jnp.float32)
    rows = [jnp.where(place == column + float(s * width), 1.0, 0.0) for s in range(sets)]
    return jnp.concatenate(rows, 0).astype(jnp.bfloat16)


def transform(records, table):
    half = table.shape[0]
    first = jnp.dot(records[:, :half], table, preferred_element_type=jnp.float32)
    second = jnp.dot(records[:, half:], table, preferred_element_type=jnp.float32)
    odd = lax.broadcasted_iota(jnp.int32, first.shape, 1) % 2
    return jnp.where(odd == 1, first - second, first + second)


def whiten(spectra):
    real_part = spectra[:, :WIDE]
    imag_part = spectra[:, WIDE:]
    square = real_part * real_part + imag_part * imag_part
    high = square.astype(jnp.bfloat16)
    low = (square - high.astype(jnp.float32)).astype(jnp.bfloat16)
    down = lax.broadcasted_iota(jnp.int32, (WIDE, WIDE), 0) // BAND
    across = lax.broadcasted_iota(jnp.int32, (WIDE, WIDE), 1) // BAND
    mean = jnp.where(down == across, 0.5 / BAND, 0.0).astype(jnp.bfloat16)
    power = jnp.dot(high, mean, preferred_element_type=jnp.float32)
    power += jnp.dot(low, mean, preferred_element_type=jnp.float32)
    factor = lax.rsqrt(power + 1e-06)
    return jnp.concatenate([real_part * factor, imag_part * factor], 1).astype(jnp.bfloat16)


def cross_sums(own, other, select, width):
    sets = own.shape[0] // width
    picked = jnp.dot(select, other, preferred_element_type=jnp.float32)
    rows = picked.shape[0] // sets
    real_sum = jnp.zeros((rows, WIDE), jnp.float32)
    imag_sum = jnp.zeros((rows, WIDE), jnp.float32)
    for s in range(sets):
        mine = own[s * width : (s + 1) * width].astype(jnp.float32)
        mine = jnp.concatenate([mine] * (rows // width), 0)
        theirs = picked[s * rows : (s + 1) * rows]
        mine_re, mine_im = mine[:, :WIDE], mine[:, WIDE:]
        their_re, their_im = theirs[:, :WIDE], theirs[:, WIDE:]
        real_sum += mine_re * their_re + mine_im * their_im
        imag_sum += mine_re * their_im - mine_im * their_re
    return jnp.concatenate([real_sum, imag_sum], 1)


def lag_terms(table, cross):
    return lax.dot_general(table, cross, (((1,), (1,)), ((), ())), preferred_element_type=jnp.float32)


def kernel(
    dims, records_hbm, visits_hbm, forward_hbm, inverse_hbm, out,
    visits, records, forward, inverse, whitened, held, held_visits, own_select, held_select, terms,
    early_out, late_out, back_out, early_in, late_in, back_in,
    load_sem, table_sem, block_send, block_recv, visit_send, visit_recv,
    early_send, early_recv, late_send, late_recv, back_send, back_recv,
):
    reach, days, segs, blocks, sets, width, picks, scale = dims
    groups = days * segs
    share = LAGS // groups
    cols = picks * width
    chan = lax.axis_index("chan")
    group = lax.axis_index("day") * segs + lax.axis_index("seg")

    def at(offset, step):
        other = lax.rem(group + step, groups)
        return {"chan": lax.rem(chan + offset + blocks, blocks), "day": other // segs, "seg": lax.rem(other, segs)}

    half = sets // 2
    halves = [(0, half), (half, sets - half)] if sets > 1 else [(0, sets)]
    parts = [(0, half), (half, sets - 1 - half), (sets - 1, 1)] if sets > 2 else halves
    pieces = [halves if c == 0 else parts if c == CHUNKS - 1 else [(0, sets)] for c in range(CHUNKS)]

    def block_rows(piece):
        return pl.ds(piece[0] * width, piece[1] * width)

    load_records = [
        pltpu.make_async_copy(records_hbm.at[block_rows(piece)], records.at[block_rows(piece)], load_sem.at[2 + i])
        for i, piece in enumerate(halves)
    ]
    load_inverse = pltpu.make_async_copy(inverse_hbm, inverse, load_sem.at[0])
    load_visits = pltpu.make_async_copy(visits_hbm, visits, load_sem.at[1])
    load_table = [
        pltpu.make_async_copy(forward_hbm.at[c], forward.at[c], table_sem.at[c]) for c in range(CHUNKS)
    ]
    load_table[0].start()
    for copy in load_records:
        copy.start()
    load_visits.start()

    barrier = pltpu.get_barrier_semaphore()
    partners = [(o, k) for o in range(-reach, reach + 1) for k in range(groups) if (o, k) != (0, 0)]
    for o, k in partners:
        pl.semaphore_signal(barrier, inc=1, device_id=at(o, k), device_id_type=MESH)
    send_visits, send_blocks = [], {}
    for c in range(CHUNKS):
        load_table[c].wait()
        for i, piece in enumerate(pieces[c]):
            if c == 0:
                load_records[i].wait()
            spectra = transform(records[block_rows(piece)], forward[c])
            whitened[c, block_rows(piece)] = whiten(spectra)
            if c == 0 and i == 0:
                load_inverse.start()
                for later in range(1, CHUNKS):
                    load_table[later].start()
                pl.semaphore_wait(barrier, len(partners))
            for o in range(1, reach + 1):
                copy = pltpu.make_async_remote_copy(
                    whitened.at[c, block_rows(piece)], held.at[o - 1, c, block_rows(piece)],
                    block_send.at[o - 1, c, i], block_recv.at[o - 1, c, i],
                    device_id=at(o, 0), device_id_type=MESH,
                )
                copy.start()
                send_blocks[c, o, i] = copy
        if c == 0:
            load_visits.wait()
            for o in range(1, reach + 1):
                copy = pltpu.make_async_remote_copy(
                    visits.at[reach - o], held_visits.at[o - 1], visit_send.at[o - 1], visit_recv.at[o - 1],
                    device_id=at(o, 0), device_id_type=MESH,
                )
                copy.start()
                send_visits.append(copy)
            for o in range(reach + 1):
                own_select[o] = selector(visits[reach + o], sets, width)
            load_inverse.wait()
        mine = whitened[c]
        cross = cross_sums(mine, mine, own_select[0], width).astype(jnp.bfloat16)
        part = lag_terms(inverse[c], cross).reshape(groups, share, cols)
        terms[reach] = part if c == 0 else terms[reach] + part

    send_results = []

    def send_result(source, target, send, recv, offset, step):
        other = lax.rem(group + step, groups)
        copy = pltpu.make_async_remote_copy(
            source.at[other], target.at[step], send.at[step], recv.at[step],
            device_id=at(offset, step), device_id_type=MESH,
        )
        copy.start()
        send_results.append(copy)
        return copy

    def finish(place, total, copies, target):
        for copy, k in copies:
            copy.wait_recv()
            total += target[k].astype(jnp.float32)
        out[:, place * cols : (place + 1) * cols] = (total * scale).astype(jnp.bfloat16)

    early_out[...] = terms[reach].astype(jnp.bfloat16)
    early = [(send_result(early_out, early_in, early_send, early_recv, 0, k), k) for k in range(1, groups)]

    for o in range(1, reach + 1):
        send_visits[o - 1].wait_recv()
        held_select[o - 1] = selector(held_visits[o - 1], sets, width)

    back, late = {}, {}
    for c in range(CHUNKS):
        if c == CHUNKS - 1:
            finish(reach, terms[reach, group], early, early_in)
        for o in range(1, reach + 1):
            up, down = 0.0, 0.0
            for i, piece in enumerate(pieces[c]):
                send_blocks[c, o, i].wait_recv()
                mine, theirs = whitened[c, block_rows(piece)], held[o - 1, c, block_rows(piece)]
                part = (slice(0, piece[1] * cols), slice(0, piece[1] * width))
                up += cross_sums(theirs, mine, held_select[o - 1][part], width)
                if c == CHUNKS - 1 and i == len(pieces[c]) - 1:
                    last = lag_terms(inverse[c], up.astype(jnp.bfloat16)).reshape(groups, share, cols)
                    back_out[o - 1] = (terms[reach - o] + last).astype(jnp.bfloat16)
                    refs = [ref.at[o - 1] for ref in (back_out, back_in, back_send, back_recv)]
                    back[o] = [(send_result(*refs, -o, k), k) for k in range(groups)]
                down += cross_sums(mine, theirs, own_select[o][part], width)
            if c < CHUNKS - 1:
                both = jnp.concatenate([down, up], 0).astype(jnp.bfloat16)
                both = lag_terms(inverse[c], both)
                for place, piece in ((reach + o, both[:, :cols]), (reach - o, both[:, cols:])):
                    piece = piece.reshape(groups, share, cols)
                    terms[place] = piece if c == 0 else terms[place] + piece
            else:
                last = lag_terms(inverse[c], down.astype(jnp.bfloat16)).reshape(groups, share, cols)
                last += terms[reach + o]
                terms[reach + o] = last
                late_out[o - 1] = last.astype(jnp.bfloat16)
                refs = [ref.at[o - 1] for ref in (late_out, late_in, late_send, late_recv)]
                late[o] = [(send_result(*refs, 0, k), k) for k in range(1, groups)]

    for o in range(1, reach + 1):
        finish(reach - o, 0.0, back[o], back_in.at[o - 1])
        finish(reach + o, terms[reach + o, group], late[o], late_in.at[o - 1])
    for copy in send_visits + list(send_blocks.values()) + send_results:
        copy.wait_send()


def local(records, visits):
    day_local, seg_local, width, samples = records.shape
    visit_count, picks, _ = visits.shape
    days, segs, blocks = lax.axis_size("day"), lax.axis_size("seg"), lax.axis_size("chan")
    reach = blocks // 4
    groups = days * segs
    share = LAGS // groups
    sets = day_local * seg_local
    rows = sets * width
    cols = picks * width
    scale = 1.0 / math.sqrt(FREQS * day_local * days * SEGS)
    bf16, f32 = jnp.bfloat16, jnp.float32
    hbm = pl.BlockSpec(memory_space=pltpu.HBM)
    vmem = pl.BlockSpec(memory_space=pltpu.VMEM)
    dma = pltpu.SemaphoreType.DMA
    flops = 2 * rows * samples * 2 * FREQS + 2 * LAGS * 2 * FREQS * visit_count * cols
    operands = (records.reshape(rows, samples), visits, forward_chunks(samples), inverse_chunks(samples))
    result = pl.pallas_call(
        functools.partial(kernel, (reach, days, segs, blocks, sets, width, picks, scale)),
        out_shape=jax.ShapeDtypeStruct((share, visit_count * cols), bf16),
        in_specs=[hbm, hbm, hbm, hbm],
        out_specs=vmem,
        scratch_shapes=[
            pltpu.VMEM((visit_count, picks, width), jnp.int32),
            pltpu.VMEM((rows, samples), bf16),
            pltpu.VMEM((CHUNKS, samples // 2, 2 * WIDE), bf16),
            pltpu.VMEM((CHUNKS, LAGS, 2 * WIDE), bf16),
            pltpu.VMEM((CHUNKS, rows, 2 * WIDE), bf16),
            pltpu.VMEM((reach, CHUNKS, rows, 2 * WIDE), bf16),
            pltpu.VMEM((reach, picks, width), jnp.int32),
            pltpu.VMEM((reach + 1, sets * cols, rows), bf16),
            pltpu.VMEM((reach, sets * cols, rows), bf16),
            pltpu.VMEM((visit_count, groups, share, cols), f32),
            pltpu.VMEM((groups, share, cols), bf16),
            pltpu.VMEM((reach, groups, share, cols), bf16),
            pltpu.VMEM((reach, groups, share, cols), bf16),
            pltpu.VMEM((groups, share, cols), bf16),
            pltpu.VMEM((reach, groups, share, cols), bf16),
            pltpu.VMEM((reach, groups, share, cols), bf16),
            dma((4,)), dma((CHUNKS,)), dma((reach, CHUNKS, 3)), dma((reach, CHUNKS, 3)), dma((reach,)), dma((reach,)),
            dma((groups,)), dma((groups,)), dma((reach, groups)), dma((reach, groups)),
            dma((reach, groups)), dma((reach, groups)),
        ],
        compiler_params=pltpu.CompilerParams(
            collective_id=0, has_side_effects=True, vmem_limit_bytes=32 * 1024 * 1024
        ),
        cost_estimate=pl.CostEstimate(flops=flops, bytes_accessed=8 * 1024 * 1024, transcendentals=0),
        name="correlate",
    )(*(pltpu.with_memory_space_constraint(jnp.asarray(x), pltpu.HBM) for x in operands))
    return result.reshape(share, visit_count, picks, width)


def solution(mesh):
    in_specs = (P("day", "seg", ("grp", "chan"), None), P(None, None, ("grp", "chan")))
    out_specs = P(("day", "seg"), None, None, ("grp", "chan"))
    return jax.shard_map(local, mesh=mesh, in_specs=in_specs, out_specs=out_specs, check_vma=False)
```

```python
import functools
import math

import jax
import jax.numpy as jnp
import ml_dtypes
import numpy as np
from jax import lax
from jax.experimental import pallas as pl
from jax.experimental.pallas import tpu as pltpu
from jax.sharding import PartitionSpec as P

FREQS = 512
BAND = 64
LAGS = 256
SEGS = 4
WIDE = 128
CHUNKS = FREQS // WIDE
MESH = pl.DeviceIdType.MESH


def forward_chunks(samples):
    index = np.arange(samples // 2)[:, None] * np.arange(FREQS)[None, :] % samples
    turns = index * (2.0 * math.pi / samples)
    table = np.stack([np.cos(turns), -np.sin(turns)], 1).reshape(samples // 2, 2, CHUNKS, WIDE)
    return table.transpose(2, 0, 1, 3).reshape(CHUNKS, samples // 2, 2 * WIDE).astype(ml_dtypes.bfloat16)


def inverse_chunks(samples):
    index = (np.arange(LAGS) - LAGS // 2)[:, None] * np.arange(FREQS)[None, :] % samples
    turns = index * (2.0 * math.pi / samples)
    table = np.stack([np.cos(turns), -np.sin(turns)], 1).reshape(LAGS, 2, CHUNKS, WIDE)
    return table.transpose(2, 0, 1, 3).reshape(CHUNKS, LAGS, 2 * WIDE).astype(ml_dtypes.bfloat16)


def selector(picks, sets, width):
    pick_count = picks.shape[0]
    across = lax.broadcasted_iota(jnp.int32, (width, width), 1)
    down = lax.broadcasted_iota(jnp.int32, (width, width), 0)
    columns = []
    for p in range(pick_count):
        row = picks[p : p + 1, :].astype(jnp.float32)
        diagonal = jnp.where(across == down, jnp.broadcast_to(row, (width, width)), 0.0)
        columns.append(jnp.sum(diagonal, axis=1, keepdims=True))
    column = jnp.concatenate(columns, 0)
    place = lax.broadcasted_iota(jnp.int32, (pick_count * width, sets * width), 1).astype(jnp.float32)
    rows = [jnp.where(place == column + float(s * width), 1.0, 0.0) for s in range(sets)]
    return jnp.concatenate(rows, 0).astype(jnp.bfloat16)


def transform(records, table):
    half = table.shape[0]
    first = jnp.dot(records[:, :half], table, preferred_element_type=jnp.float32)
    second = jnp.dot(records[:, half:], table, preferred_element_type=jnp.float32)
    odd = lax.broadcasted_iota(jnp.int32, first.shape, 1) % 2
    return jnp.where(odd == 1, first - second, first + second)


def whiten(spectra):
    real_part = spectra[:, :WIDE]
    imag_part = spectra[:, WIDE:]
    square = real_part * real_part + imag_part * imag_part
    high = square.astype(jnp.bfloat16)
    low = (square - high.astype(jnp.float32)).astype(jnp.bfloat16)
    down = lax.broadcasted_iota(jnp.int32, (WIDE, WIDE), 0) // BAND
    across = lax.broadcasted_iota(jnp.int32, (WIDE, WIDE), 1) // BAND
    mean = jnp.where(down == across, 0.5 / BAND, 0.0).astype(jnp.bfloat16)
    power = jnp.dot(high, mean, preferred_element_type=jnp.float32)
    power += jnp.dot(low, mean, preferred_element_type=jnp.float32)
    factor = lax.rsqrt(power + 1e-06)
    return jnp.concatenate([real_part * factor, imag_part * factor], 1).astype(jnp.bfloat16)


def cross_sums(own, other, select, width):
    sets = own.shape[0] // width
    picked = jnp.dot(select, other, preferred_element_type=jnp.float32)
    rows = picked.shape[0] // sets
    real_sum = jnp.zeros((rows, WIDE), jnp.float32)
    imag_sum = jnp.zeros((rows, WIDE), jnp.float32)
    for s in range(sets):
        mine = own[s * width : (s + 1) * width].astype(jnp.float32)
        mine = jnp.concatenate([mine] * (rows // width), 0)
        theirs = picked[s * rows : (s + 1) * rows]
        mine_re, mine_im = mine[:, :WIDE], mine[:, WIDE:]
        their_re, their_im = theirs[:, :WIDE], theirs[:, WIDE:]
        real_sum += mine_re * their_re + mine_im * their_im
        imag_sum += mine_re * their_im - mine_im * their_re
    return jnp.concatenate([real_sum, imag_sum], 1)


def lag_terms(table, cross):
    return lax.dot_general(table, cross, (((1,), (1,)), ((), ())), preferred_element_type=jnp.float32)


def kernel(
    dims, records_hbm, visits_hbm, forward_hbm, inverse_hbm, out,
    visits, records, forward, inverse, whitened, held, held_visits, own_select, held_select, terms,
    early_out, late_out, back_out, early_in, late_in, back_in,
    load_sem, table_sem, block_send, block_recv, visit_send, visit_recv,
    early_send, early_recv, late_send, late_recv, back_send, back_recv,
):
    reach, days, segs, blocks, sets, width, picks, scale = dims
    groups = days * segs
    share = LAGS // groups
    cols = picks * width
    chan = lax.axis_index("chan")
    group = lax.axis_index("day") * segs + lax.axis_index("seg")

    def at(offset, step):
        other = lax.rem(group + step, groups)
        return {"chan": lax.rem(chan + offset + blocks, blocks), "day": other // segs, "seg": lax.rem(other, segs)}

    half = sets // 2
    halves = [(0, half), (half, sets - half)] if sets > 1 else [(0, sets)]
    parts = [(0, half), (half, sets - 1 - half), (sets - 1, 1)] if sets > 2 else halves
    pieces = [halves if c == 0 else parts if c == CHUNKS - 1 else [(0, sets)] for c in range(CHUNKS)]

    def block_rows(piece):
        return pl.ds(piece[0] * width, piece[1] * width)

    load_records = [
        pltpu.make_async_copy(records_hbm.at[block_rows(piece)], records.at[block_rows(piece)], load_sem.at[2 + i])
        for i, piece in enumerate(halves)
    ]
    load_inverse = pltpu.make_async_copy(inverse_hbm, inverse, load_sem.at[0])
    load_visits = pltpu.make_async_copy(visits_hbm, visits, load_sem.at[1])
    load_table = [
        pltpu.make_async_copy(forward_hbm.at[c], forward.at[c], table_sem.at[c]) for c in range(CHUNKS)
    ]
    load_table[0].start()
    for copy in load_records:
        copy.start()
    load_visits.start()

    barrier = pltpu.get_barrier_semaphore()
    partners = [(o, k) for o in range(-reach, reach + 1) for k in range(groups) if (o, k) != (0, 0)]
    for o, k in partners:
        pl.semaphore_signal(barrier, inc=1, device_id=at(o, k), device_id_type=MESH)
    order = [(c, i) for c in range(CHUNKS) for i in range(len(pieces[c]))]
    send_visits, send_blocks, sent = [], {}, set()

    def left(c, i):
        for o in range(1, reach + 1):
            if (c, o, i) not in sent:
                sent.add((c, o, i))
                send_blocks[c, o, i].wait_send()

    def send_piece(c, i):
        place = order.index((c, i))
        if place >= 2:
            left(*order[place - 2])
        rows = block_rows(pieces[c][i])
        for o in range(1, reach + 1):
            copy = pltpu.make_async_remote_copy(
                whitened.at[c, rows], held.at[o - 1, c, rows],
                block_send.at[o - 1, c, i], block_recv.at[o - 1, c, i],
                device_id=at(o, 0), device_id_type=MESH,
            )
            copy.start()
            send_blocks[c, o, i] = copy

    def own_visit(c):
        mine = whitened[c]
        cross = cross_sums(mine, mine, own_select[0], width).astype(jnp.bfloat16)
        part = lag_terms(inverse[c], cross).reshape(groups, share, cols)
        terms[reach] = part if c == 0 else terms[reach] + part

    send_results = []

    def send_result(source, target, send, recv, offset, step):
        other = lax.rem(group + step, groups)
        copy = pltpu.make_async_remote_copy(
            source.at[other], target.at[step], send.at[step], recv.at[step],
            device_id=at(offset, step), device_id_type=MESH,
        )
        copy.start()
        send_results.append(copy)
        return copy

    def finish(place, total, copies, target):
        for copy, k in copies:
            copy.wait_recv()
            total += target[k].astype(jnp.float32)
        out[:, place * cols : (place + 1) * cols] = (total * scale).astype(jnp.bfloat16)

    back, late = {}, {}

    def held_visits_of(c):
        for o in range(1, reach + 1):
            up, down = 0.0, 0.0
            for i, piece in enumerate(pieces[c]):
                send_blocks[c, o, i].wait_recv()
                mine, theirs = whitened[c, block_rows(piece)], held[o - 1, c, block_rows(piece)]
                part = (slice(0, piece[1] * cols), slice(0, piece[1] * width))
                up += cross_sums(theirs, mine, held_select[o - 1][part], width)
                if c == CHUNKS - 1 and i == len(pieces[c]) - 1:
                    last = lag_terms(inverse[c], up.astype(jnp.bfloat16)).reshape(groups, share, cols)
                    back_out[o - 1] = (terms[reach - o] + last).astype(jnp.bfloat16)
                    refs = [ref.at[o - 1] for ref in (back_out, back_in, back_send, back_recv)]
                    back[o] = [(send_result(*refs, -o, k), k) for k in range(groups)]
                down += cross_sums(mine, theirs, own_select[o][part], width)
            if c < CHUNKS - 1:
                both = jnp.concatenate([down, up], 0).astype(jnp.bfloat16)
                both = lag_terms(inverse[c], both)
                for place, piece in ((reach + o, both[:, :cols]), (reach - o, both[:, cols:])):
                    piece = piece.reshape(groups, share, cols)
                    terms[place] = piece if c == 0 else terms[place] + piece
            else:
                last = lag_terms(inverse[c], down.astype(jnp.bfloat16)).reshape(groups, share, cols)
                last += terms[reach + o]
                terms[reach + o] = last
                late_out[o - 1] = last.astype(jnp.bfloat16)
                refs = [ref.at[o - 1] for ref in (late_out, late_in, late_send, late_recv)]
                late[o] = [(send_result(*refs, 0, k), k) for k in range(1, groups)]

    for i, piece in enumerate(pieces[0]):
        if i == 0:
            load_table[0].wait()
        load_records[i].wait()
        whitened[0, block_rows(piece)] = whiten(transform(records[block_rows(piece)], forward[0]))
        if i == 0:
            for later in range(1, CHUNKS):
                load_table[later].start()
            load_inverse.start()
            pl.semaphore_wait(barrier, len(partners))
        send_piece(0, i)
    load_visits.wait()
    for o in range(1, reach + 1):
        copy = pltpu.make_async_remote_copy(
            visits.at[reach - o], held_visits.at[o - 1], visit_send.at[o - 1], visit_recv.at[o - 1],
            device_id=at(o, 0), device_id_type=MESH,
        )
        copy.start()
        send_visits.append(copy)
    for c in range(1, CHUNKS):
        load_table[c].wait()
        whitened[c] = whiten(transform(records[...], forward[c]))
        if c == 1:
            for o in range(reach + 1):
                own_select[o] = selector(visits[reach + o], sets, width)
            load_inverse.wait()
        own_visit(c - 1)
        if c < CHUNKS - 1:
            for i in range(len(pieces[c])):
                send_piece(c, i)
    own_visit(CHUNKS - 1)

    early_out[...] = terms[reach].astype(jnp.bfloat16)
    early = [(send_result(early_out, early_in, early_send, early_recv, 0, k), k) for k in range(1, groups)]

    for o in range(1, reach + 1):
        send_visits[o - 1].wait_recv()
        held_select[o - 1] = selector(held_visits[o - 1], sets, width)

    for c in range(CHUNKS):
        held_visits_of(c)
        if c < CHUNKS - 1 and c < len(pieces[-1]):
            send_piece(CHUNKS - 1, c)
        if c == CHUNKS - 2:
            for i in range(CHUNKS - 1, len(pieces[-1])):
                send_piece(CHUNKS - 1, i)
            finish(reach, terms[reach, group], early, early_in)

    for o in range(1, reach + 1):
        finish(reach - o, 0.0, back[o], back_in.at[o - 1])
        finish(reach + o, terms[reach + o, group], late[o], late_in.at[o - 1])
    for piece in order:
        left(*piece)
    for copy in send_visits + send_results:
        copy.wait_send()


def local(records, visits):
    day_local, seg_local, width, samples = records.shape
    visit_count, picks, _ = visits.shape
    days, segs, blocks = lax.axis_size("day"), lax.axis_size("seg"), lax.axis_size("chan")
    reach = blocks // 4
    groups = days * segs
    share = LAGS // groups
    sets = day_local * seg_local
    rows = sets * width
    cols = picks * width
    scale = 1.0 / math.sqrt(FREQS * day_local * days * SEGS)
    bf16, f32 = jnp.bfloat16, jnp.float32
    hbm = pl.BlockSpec(memory_space=pltpu.HBM)
    vmem = pl.BlockSpec(memory_space=pltpu.VMEM)
    dma = pltpu.SemaphoreType.DMA
    flops = 2 * rows * samples * 2 * FREQS + 2 * LAGS * 2 * FREQS * visit_count * cols
    operands = (records.reshape(rows, samples), visits, forward_chunks(samples), inverse_chunks(samples))
    result = pl.pallas_call(
        functools.partial(kernel, (reach, days, segs, blocks, sets, width, picks, scale)),
        out_shape=jax.ShapeDtypeStruct((share, visit_count * cols), bf16),
        in_specs=[hbm, hbm, hbm, hbm],
        out_specs=vmem,
        scratch_shapes=[
            pltpu.VMEM((visit_count, picks, width), jnp.int32),
            pltpu.VMEM((rows, samples), bf16),
            pltpu.VMEM((CHUNKS, samples // 2, 2 * WIDE), bf16),
            pltpu.VMEM((CHUNKS, LAGS, 2 * WIDE), bf16),
            pltpu.VMEM((CHUNKS, rows, 2 * WIDE), bf16),
            pltpu.VMEM((reach, CHUNKS, rows, 2 * WIDE), bf16),
            pltpu.VMEM((reach, picks, width), jnp.int32),
            pltpu.VMEM((reach + 1, sets * cols, rows), bf16),
            pltpu.VMEM((reach, sets * cols, rows), bf16),
            pltpu.VMEM((visit_count, groups, share, cols), f32),
            pltpu.VMEM((groups, share, cols), bf16),
            pltpu.VMEM((reach, groups, share, cols), bf16),
            pltpu.VMEM((reach, groups, share, cols), bf16),
            pltpu.VMEM((groups, share, cols), bf16),
            pltpu.VMEM((reach, groups, share, cols), bf16),
            pltpu.VMEM((reach, groups, share, cols), bf16),
            dma((4,)), dma((CHUNKS,)), dma((reach, CHUNKS, 3)), dma((reach, CHUNKS, 3)), dma((reach,)), dma((reach,)),
            dma((groups,)), dma((groups,)), dma((reach, groups)), dma((reach, groups)),
            dma((reach, groups)), dma((reach, groups)),
        ],
        compiler_params=pltpu.CompilerParams(
            collective_id=0, has_side_effects=True, vmem_limit_bytes=32 * 1024 * 1024
        ),
        cost_estimate=pl.CostEstimate(flops=flops, bytes_accessed=8 * 1024 * 1024, transcendentals=0),
        name="correlate",
    )(*(pltpu.with_memory_space_constraint(jnp.asarray(x), pltpu.HBM) for x in operands))
    return result.reshape(share, visit_count, picks, width)


def solution(mesh):
    in_specs = (P("day", "seg", ("grp", "chan"), None), P(None, None, ("grp", "chan")))
    out_specs = P(("day", "seg"), None, None, ("grp", "chan"))
    return jax.shard_map(local, mesh=mesh, in_specs=in_specs, out_specs=out_specs, check_vma=False)
```

```python
import functools
import math

import jax
import jax.numpy as jnp
import ml_dtypes
import numpy as np
from jax import lax
from jax.experimental import pallas as pl
from jax.experimental.pallas import tpu as pltpu
from jax.sharding import PartitionSpec as P

FREQS = 512
BAND = 64
LAGS = 256
SEGS = 4
WIDE = 128
CHUNKS = FREQS // WIDE
MESH = pl.DeviceIdType.MESH


def forward_chunks(samples):
    index = np.arange(samples // 2)[:, None] * np.arange(FREQS)[None, :] % samples
    turns = index * (2.0 * math.pi / samples)
    table = np.stack([np.cos(turns), -np.sin(turns)], 1).reshape(samples // 2, 2, CHUNKS, WIDE)
    return table.transpose(2, 0, 1, 3).reshape(CHUNKS, samples // 2, 2 * WIDE).astype(ml_dtypes.bfloat16)


def inverse_chunks(samples):
    index = (np.arange(LAGS) - LAGS // 2)[:, None] * np.arange(FREQS)[None, :] % samples
    turns = index * (2.0 * math.pi / samples)
    table = np.stack([np.cos(turns), -np.sin(turns)], 1).reshape(LAGS, 2, CHUNKS, WIDE)
    return table.transpose(2, 0, 1, 3).reshape(CHUNKS, LAGS, 2 * WIDE).astype(ml_dtypes.bfloat16)


def selector(picks, sets, width):
    pick_count = picks.shape[0]
    across = lax.broadcasted_iota(jnp.int32, (width, width), 1)
    down = lax.broadcasted_iota(jnp.int32, (width, width), 0)
    columns = []
    for p in range(pick_count):
        row = picks[p : p + 1, :].astype(jnp.float32)
        diagonal = jnp.where(across == down, jnp.broadcast_to(row, (width, width)), 0.0)
        columns.append(jnp.sum(diagonal, axis=1, keepdims=True))
    column = jnp.concatenate(columns, 0)
    place = lax.broadcasted_iota(jnp.int32, (pick_count * width, sets * width), 1).astype(jnp.float32)
    rows = [jnp.where(place == column + float(s * width), 1.0, 0.0) for s in range(sets)]
    return jnp.concatenate(rows, 0).astype(jnp.bfloat16)


def transform(records, table):
    half = table.shape[0]
    first = jnp.dot(records[:, :half], table, preferred_element_type=jnp.float32)
    second = jnp.dot(records[:, half:], table, preferred_element_type=jnp.float32)
    odd = lax.broadcasted_iota(jnp.int32, first.shape, 1) % 2
    return jnp.where(odd == 1, first - second, first + second)


def whiten(spectra):
    real_part = spectra[:, :WIDE]
    imag_part = spectra[:, WIDE:]
    square = real_part * real_part + imag_part * imag_part
    high = square.astype(jnp.bfloat16)
    low = (square - high.astype(jnp.float32)).astype(jnp.bfloat16)
    down = lax.broadcasted_iota(jnp.int32, (WIDE, WIDE), 0) // BAND
    across = lax.broadcasted_iota(jnp.int32, (WIDE, WIDE), 1) // BAND
    mean = jnp.where(down == across, 0.5 / BAND, 0.0).astype(jnp.bfloat16)
    power = jnp.dot(high, mean, preferred_element_type=jnp.float32)
    power += jnp.dot(low, mean, preferred_element_type=jnp.float32)
    factor = lax.rsqrt(power + 1e-06)
    return jnp.concatenate([real_part * factor, imag_part * factor], 1).astype(jnp.bfloat16)


def cross_sums(own, other, select, width):
    sets = own.shape[0] // width
    picked = jnp.dot(select, other, preferred_element_type=jnp.float32)
    rows = picked.shape[0] // sets
    real_sum = jnp.zeros((rows, WIDE), jnp.float32)
    imag_sum = jnp.zeros((rows, WIDE), jnp.float32)
    for s in range(sets):
        mine = own[s * width : (s + 1) * width].astype(jnp.float32)
        mine = jnp.concatenate([mine] * (rows // width), 0)
        theirs = picked[s * rows : (s + 1) * rows]
        mine_re, mine_im = mine[:, :WIDE], mine[:, WIDE:]
        their_re, their_im = theirs[:, :WIDE], theirs[:, WIDE:]
        real_sum += mine_re * their_re + mine_im * their_im
        imag_sum += mine_re * their_im - mine_im * their_re
    return jnp.concatenate([real_sum, imag_sum], 1)


def lag_terms(table, cross):
    return lax.dot_general(table, cross, (((1,), (1,)), ((), ())), preferred_element_type=jnp.float32)


def kernel(
    dims, records_hbm, visits_hbm, forward_hbm, inverse_hbm, out,
    visits, records, forward, inverse, whitened, held, held_visits, own_select, held_select, terms,
    early_out, late_out, back_out, early_in, late_in, back_in,
    load_sem, table_sem, block_send, block_recv, visit_send, visit_recv,
    early_send, early_recv, late_send, late_recv, back_send, back_recv,
):
    reach, days, segs, blocks, sets, width, picks, scale = dims
    groups = days * segs
    share = LAGS // groups
    cols = picks * width
    chan = lax.axis_index("chan")
    group = lax.axis_index("day") * segs + lax.axis_index("seg")

    def at(offset, step):
        other = lax.rem(group + step, groups)
        return {"chan": lax.rem(chan + offset + blocks, blocks), "day": other // segs, "seg": lax.rem(other, segs)}

    half = sets // 2
    halves = [(0, half), (half, sets - half)] if sets > 1 else [(0, sets)]
    parts = [(0, half), (half, sets - 1 - half), (sets - 1, 1)] if sets > 2 else halves
    pieces = [parts if c == CHUNKS - 1 else halves for c in range(CHUNKS)]

    def block_rows(piece):
        return pl.ds(piece[0] * width, piece[1] * width)

    load_records = [
        pltpu.make_async_copy(records_hbm.at[block_rows(piece)], records.at[block_rows(piece)], load_sem.at[2 + i])
        for i, piece in enumerate(halves)
    ]
    load_inverse = pltpu.make_async_copy(inverse_hbm, inverse, load_sem.at[0])
    load_visits = pltpu.make_async_copy(visits_hbm, visits, load_sem.at[1])
    load_table = [
        pltpu.make_async_copy(forward_hbm.at[c], forward.at[c], table_sem.at[c]) for c in range(CHUNKS)
    ]
    load_table[0].start()
    for copy in load_records:
        copy.start()
    load_visits.start()

    barrier = pltpu.get_barrier_semaphore()
    partners = [(o, k) for o in range(-reach, reach + 1) for k in range(groups) if (o, k) != (0, 0)]
    for o, k in partners:
        pl.semaphore_signal(barrier, inc=1, device_id=at(o, k), device_id_type=MESH)
    send_visits, send_blocks = [], {}

    def send_piece(c, i):
        rows = block_rows(pieces[c][i])
        for o in range(1, reach + 1):
            copy = pltpu.make_async_remote_copy(
                whitened.at[c, rows], held.at[o - 1, c, rows],
                block_send.at[o - 1, c, i], block_recv.at[o - 1, c, i],
                device_id=at(o, 0), device_id_type=MESH,
            )
            copy.start()
            send_blocks[c, o, i] = copy

    def own_visit(c):
        mine = whitened[c]
        cross = cross_sums(mine, mine, own_select[0], width).astype(jnp.bfloat16)
        part = lag_terms(inverse[c], cross).reshape(groups, share, cols)
        terms[reach] = part if c == 0 else terms[reach] + part

    send_results = []

    def send_result(source, target, send, recv, offset, step):
        other = lax.rem(group + step, groups)
        copy = pltpu.make_async_remote_copy(
            source.at[other], target.at[step], send.at[step], recv.at[step],
            device_id=at(offset, step), device_id_type=MESH,
        )
        copy.start()
        send_results.append(copy)
        return copy

    def finish(place, total, copies, target):
        for copy, k in copies:
            copy.wait_recv()
            total += target[k].astype(jnp.float32)
        out[:, place * cols : (place + 1) * cols] = (total * scale).astype(jnp.bfloat16)

    back, late = {}, {}

    def held_visits_of(c):
        for o in range(1, reach + 1):
            up, down = 0.0, 0.0
            work = pieces[c] if c == CHUNKS - 1 else [(0, sets)]
            for i, piece in enumerate(work):
                for j in range(len(pieces[c])) if c < CHUNKS - 1 else [i]:
                    send_blocks[c, o, j].wait_recv()
                mine, theirs = whitened[c, block_rows(piece)], held[o - 1, c, block_rows(piece)]
                part = (slice(0, piece[1] * cols), slice(0, piece[1] * width))
                up += cross_sums(theirs, mine, held_select[o - 1][part], width)
                if c == CHUNKS - 1 and i == len(pieces[c]) - 1:
                    last = lag_terms(inverse[c], up.astype(jnp.bfloat16)).reshape(groups, share, cols)
                    back_out[o - 1] = (terms[reach - o] + last).astype(jnp.bfloat16)
                    refs = [ref.at[o - 1] for ref in (back_out, back_in, back_send, back_recv)]
                    back[o] = [(send_result(*refs, -o, k), k) for k in range(groups)]
                down += cross_sums(mine, theirs, own_select[o][part], width)
            if c < CHUNKS - 1:
                both = jnp.concatenate([down, up], 0).astype(jnp.bfloat16)
                both = lag_terms(inverse[c], both)
                for place, piece in ((reach + o, both[:, :cols]), (reach - o, both[:, cols:])):
                    piece = piece.reshape(groups, share, cols)
                    terms[place] = piece if c == 0 else terms[place] + piece
            else:
                last = lag_terms(inverse[c], down.astype(jnp.bfloat16)).reshape(groups, share, cols)
                last += terms[reach + o]
                terms[reach + o] = last
                late_out[o - 1] = last.astype(jnp.bfloat16)
                refs = [ref.at[o - 1] for ref in (late_out, late_in, late_send, late_recv)]
                late[o] = [(send_result(*refs, 0, k), k) for k in range(1, groups)]

    for i, piece in enumerate(pieces[0]):
        if i == 0:
            load_table[0].wait()
        load_records[i].wait()
        whitened[0, block_rows(piece)] = whiten(transform(records[block_rows(piece)], forward[0]))
        if i == 0:
            for later in range(1, CHUNKS):
                load_table[later].start()
            load_inverse.start()
            pl.semaphore_wait(barrier, len(partners))
        send_piece(0, i)
    load_visits.wait()
    for o in range(1, reach + 1):
        copy = pltpu.make_async_remote_copy(
            visits.at[reach - o], held_visits.at[o - 1], visit_send.at[o - 1], visit_recv.at[o - 1],
            device_id=at(o, 0), device_id_type=MESH,
        )
        copy.start()
        send_visits.append(copy)
    for c in range(1, CHUNKS):
        load_table[c].wait()
        for i, piece in enumerate(pieces[c]):
            whitened[c, block_rows(piece)] = whiten(transform(records[block_rows(piece)], forward[c]))
            send_piece(c, i)
    for o in range(reach + 1):
        own_select[o] = selector(visits[reach + o], sets, width)
    load_inverse.wait()
    for c in range(CHUNKS):
        own_visit(c)

    early_out[...] = terms[reach].astype(jnp.bfloat16)
    early = [(send_result(early_out, early_in, early_send, early_recv, 0, k), k) for k in range(1, groups)]

    for o in range(1, reach + 1):
        send_visits[o - 1].wait_recv()
        held_select[o - 1] = selector(held_visits[o - 1], sets, width)

    for c in range(CHUNKS):
        if c == CHUNKS - 1:
            finish(reach, terms[reach, group], early, early_in)
        held_visits_of(c)

    for o in range(1, reach + 1):
        finish(reach - o, 0.0, back[o], back_in.at[o - 1])
        finish(reach + o, terms[reach + o, group], late[o], late_in.at[o - 1])
    for copy in send_visits + list(send_blocks.values()) + send_results:
        copy.wait_send()


def local(records, visits):
    day_local, seg_local, width, samples = records.shape
    visit_count, picks, _ = visits.shape
    days, segs, blocks = lax.axis_size("day"), lax.axis_size("seg"), lax.axis_size("chan")
    reach = blocks // 4
    groups = days * segs
    share = LAGS // groups
    sets = day_local * seg_local
    rows = sets * width
    cols = picks * width
    scale = 1.0 / math.sqrt(FREQS * day_local * days * SEGS)
    bf16, f32 = jnp.bfloat16, jnp.float32
    hbm = pl.BlockSpec(memory_space=pltpu.HBM)
    vmem = pl.BlockSpec(memory_space=pltpu.VMEM)
    dma = pltpu.SemaphoreType.DMA
    flops = 2 * rows * samples * 2 * FREQS + 2 * LAGS * 2 * FREQS * visit_count * cols
    operands = (records.reshape(rows, samples), visits, forward_chunks(samples), inverse_chunks(samples))
    result = pl.pallas_call(
        functools.partial(kernel, (reach, days, segs, blocks, sets, width, picks, scale)),
        out_shape=jax.ShapeDtypeStruct((share, visit_count * cols), bf16),
        in_specs=[hbm, hbm, hbm, hbm],
        out_specs=vmem,
        scratch_shapes=[
            pltpu.VMEM((visit_count, picks, width), jnp.int32),
            pltpu.VMEM((rows, samples), bf16),
            pltpu.VMEM((CHUNKS, samples // 2, 2 * WIDE), bf16),
            pltpu.VMEM((CHUNKS, LAGS, 2 * WIDE), bf16),
            pltpu.VMEM((CHUNKS, rows, 2 * WIDE), bf16),
            pltpu.VMEM((reach, CHUNKS, rows, 2 * WIDE), bf16),
            pltpu.VMEM((reach, picks, width), jnp.int32),
            pltpu.VMEM((reach + 1, sets * cols, rows), bf16),
            pltpu.VMEM((reach, sets * cols, rows), bf16),
            pltpu.VMEM((visit_count, groups, share, cols), f32),
            pltpu.VMEM((groups, share, cols), bf16),
            pltpu.VMEM((reach, groups, share, cols), bf16),
            pltpu.VMEM((reach, groups, share, cols), bf16),
            pltpu.VMEM((groups, share, cols), bf16),
            pltpu.VMEM((reach, groups, share, cols), bf16),
            pltpu.VMEM((reach, groups, share, cols), bf16),
            dma((4,)), dma((CHUNKS,)), dma((reach, CHUNKS, 3)), dma((reach, CHUNKS, 3)), dma((reach,)), dma((reach,)),
            dma((groups,)), dma((groups,)), dma((reach, groups)), dma((reach, groups)),
            dma((reach, groups)), dma((reach, groups)),
        ],
        compiler_params=pltpu.CompilerParams(
            collective_id=0, has_side_effects=True, vmem_limit_bytes=32 * 1024 * 1024
        ),
        cost_estimate=pl.CostEstimate(flops=flops, bytes_accessed=8 * 1024 * 1024, transcendentals=0),
        name="correlate",
    )(*(pltpu.with_memory_space_constraint(jnp.asarray(x), pltpu.HBM) for x in operands))
    return result.reshape(share, visit_count, picks, width)


def solution(mesh):
    in_specs = (P("day", "seg", ("grp", "chan"), None), P(None, None, ("grp", "chan")))
    out_specs = P(("day", "seg"), None, None, ("grp", "chan"))
    return jax.shard_map(local, mesh=mesh, in_specs=in_specs, out_specs=out_specs, check_vma=False)
```

```python
import functools
import math

import jax
import jax.numpy as jnp
import ml_dtypes
import numpy as np
from jax import lax
from jax.experimental import pallas as pl
from jax.experimental.pallas import tpu as pltpu
from jax.sharding import PartitionSpec as P

FREQS = 512
BAND = 64
LAGS = 256
SEGS = 4
WIDE = 128
CHUNKS = FREQS // WIDE
MESH = pl.DeviceIdType.MESH


def forward_chunks(samples):
    index = np.arange(samples // 2)[:, None] * np.arange(FREQS)[None, :] % samples
    turns = index * (2.0 * math.pi / samples)
    table = np.stack([np.cos(turns), -np.sin(turns)], 1).reshape(samples // 2, 2, CHUNKS, WIDE)
    return table.transpose(2, 0, 1, 3).reshape(CHUNKS, samples // 2, 2 * WIDE).astype(ml_dtypes.bfloat16)


def inverse_chunks(samples):
    index = (np.arange(LAGS) - LAGS // 2)[:, None] * np.arange(FREQS)[None, :] % samples
    turns = index * (2.0 * math.pi / samples)
    table = np.stack([np.cos(turns), -np.sin(turns)], 1).reshape(LAGS, 2, CHUNKS, WIDE)
    return table.transpose(2, 0, 1, 3).reshape(CHUNKS, LAGS, 2 * WIDE).astype(ml_dtypes.bfloat16)


def selector(picks, sets, width):
    pick_count = picks.shape[0]
    across = lax.broadcasted_iota(jnp.int32, (width, width), 1)
    down = lax.broadcasted_iota(jnp.int32, (width, width), 0)
    columns = []
    for p in range(pick_count):
        row = picks[p : p + 1, :].astype(jnp.float32)
        diagonal = jnp.where(across == down, jnp.broadcast_to(row, (width, width)), 0.0)
        columns.append(jnp.sum(diagonal, axis=1, keepdims=True))
    column = jnp.concatenate(columns, 0)
    place = lax.broadcasted_iota(jnp.int32, (pick_count * width, sets * width), 1).astype(jnp.float32)
    rows = [jnp.where(place == column + float(s * width), 1.0, 0.0) for s in range(sets)]
    return jnp.concatenate(rows, 0).astype(jnp.bfloat16)


def transform(records, table):
    half = table.shape[0]
    first = jnp.dot(records[:, :half], table, preferred_element_type=jnp.float32)
    second = jnp.dot(records[:, half:], table, preferred_element_type=jnp.float32)
    odd = lax.broadcasted_iota(jnp.int32, first.shape, 1) % 2
    return jnp.where(odd == 1, first - second, first + second)


def whiten(spectra):
    real_part = spectra[:, :WIDE]
    imag_part = spectra[:, WIDE:]
    square = real_part * real_part + imag_part * imag_part
    high = square.astype(jnp.bfloat16)
    low = (square - high.astype(jnp.float32)).astype(jnp.bfloat16)
    down = lax.broadcasted_iota(jnp.int32, (WIDE, WIDE), 0) // BAND
    across = lax.broadcasted_iota(jnp.int32, (WIDE, WIDE), 1) // BAND
    mean = jnp.where(down == across, 0.5 / BAND, 0.0).astype(jnp.bfloat16)
    power = jnp.dot(high, mean, preferred_element_type=jnp.float32)
    power += jnp.dot(low, mean, preferred_element_type=jnp.float32)
    factor = lax.rsqrt(power + 1e-06)
    return jnp.concatenate([real_part * factor, imag_part * factor], 1).astype(jnp.bfloat16)


def cross_sums(own, other, select, width):
    sets = own.shape[0] // width
    picked = jnp.dot(select, other, preferred_element_type=jnp.float32)
    rows = picked.shape[0] // sets
    real_sum = jnp.zeros((rows, WIDE), jnp.float32)
    imag_sum = jnp.zeros((rows, WIDE), jnp.float32)
    for s in range(sets):
        mine = own[s * width : (s + 1) * width].astype(jnp.float32)
        mine = jnp.concatenate([mine] * (rows // width), 0)
        theirs = picked[s * rows : (s + 1) * rows]
        mine_re, mine_im = mine[:, :WIDE], mine[:, WIDE:]
        their_re, their_im = theirs[:, :WIDE], theirs[:, WIDE:]
        real_sum += mine_re * their_re + mine_im * their_im
        imag_sum += mine_re * their_im - mine_im * their_re
    return jnp.concatenate([real_sum, imag_sum], 1)


def lag_terms(table, cross):
    return lax.dot_general(table, cross, (((1,), (1,)), ((), ())), preferred_element_type=jnp.float32)


def kernel(
    dims, records_hbm, visits_hbm, forward_hbm, inverse_hbm, out,
    visits, records, forward, inverse, whitened, held, held_visits, own_select, held_select, terms,
    early_out, late_out, back_out, early_in, late_in, back_in,
    load_sem, table_sem, block_send, block_recv, visit_send, visit_recv,
    early_send, early_recv, late_send, late_recv, back_send, back_recv,
):
    reach, days, segs, blocks, sets, width, picks, scale = dims
    groups = days * segs
    share = LAGS // groups
    cols = picks * width
    chan = lax.axis_index("chan")
    group = lax.axis_index("day") * segs + lax.axis_index("seg")

    def at(offset, step):
        other = lax.rem(group + step, groups)
        return {"chan": lax.rem(chan + offset + blocks, blocks), "day": other // segs, "seg": lax.rem(other, segs)}

    half = sets // 2
    halves = [(0, half), (half, sets - half)] if sets > 1 else [(0, sets)]
    parts = [(0, half), (half, sets - 1 - half), (sets - 1, 1)] if sets > 2 else halves
    pieces = [parts if c == CHUNKS - 1 else halves for c in range(CHUNKS)]

    def block_rows(piece):
        return pl.ds(piece[0] * width, piece[1] * width)

    load_records = [
        pltpu.make_async_copy(records_hbm.at[block_rows(piece)], records.at[block_rows(piece)], load_sem.at[2 + i])
        for i, piece in enumerate(halves)
    ]
    load_inverse = pltpu.make_async_copy(inverse_hbm, inverse, load_sem.at[0])
    load_visits = pltpu.make_async_copy(visits_hbm, visits, load_sem.at[1])
    load_table = [
        pltpu.make_async_copy(forward_hbm.at[c], forward.at[c], table_sem.at[c]) for c in range(CHUNKS)
    ]
    load_table[0].start()
    for copy in load_records:
        copy.start()
    load_visits.start()

    barrier = pltpu.get_barrier_semaphore()
    partners = [(o, k) for o in range(-reach, reach + 1) for k in range(groups) if (o, k) != (0, 0)]
    for o, k in partners:
        pl.semaphore_signal(barrier, inc=1, device_id=at(o, k), device_id_type=MESH)
    send_visits, send_blocks = [], {}

    def send_piece(c, i):
        rows = block_rows(pieces[c][i])
        for o in range(1, reach + 1):
            copy = pltpu.make_async_remote_copy(
                whitened.at[c, rows], held.at[o - 1, c, rows],
                block_send.at[o - 1, c, i], block_recv.at[o - 1, c, i],
                device_id=at(o, 0), device_id_type=MESH,
            )
            copy.start()
            send_blocks[c, o, i] = copy

    def own_visit(c):
        mine = whitened[c]
        cross = cross_sums(mine, mine, own_select[0], width).astype(jnp.bfloat16)
        part = lag_terms(inverse[c], cross).reshape(groups, share, cols)
        terms[reach] = part if c == 0 else terms[reach] + part

    send_results = []

    def send_result(source, target, send, recv, offset, step):
        other = lax.rem(group + step, groups)
        copy = pltpu.make_async_remote_copy(
            source.at[other], target.at[step], send.at[step], recv.at[step],
            device_id=at(offset, step), device_id_type=MESH,
        )
        copy.start()
        send_results.append(copy)
        return copy

    def finish(place, total, copies, target):
        for copy, k in copies:
            copy.wait_recv()
            total += target[k].astype(jnp.float32)
        out[:, place * cols : (place + 1) * cols] = (total * scale).astype(jnp.bfloat16)

    back, late = {}, {}

    def held_visits_of(c):
        for o in range(1, reach + 1):
            up, down = 0.0, 0.0
            work = pieces[c] if c == CHUNKS - 1 else [(0, sets)]
            for i, piece in enumerate(work):
                for j in range(len(pieces[c])) if c < CHUNKS - 1 else [i]:
                    send_blocks[c, o, j].wait_recv()
                mine, theirs = whitened[c, block_rows(piece)], held[o - 1, c, block_rows(piece)]
                part = (slice(0, piece[1] * cols), slice(0, piece[1] * width))
                down += cross_sums(mine, theirs, own_select[o][part], width)
                if c == CHUNKS - 1 and i == len(work) - 1:
                    last = lag_terms(inverse[c], down.astype(jnp.bfloat16)).reshape(groups, share, cols)
                    last += terms[reach + o]
                    terms[reach + o] = last
                    late_out[o - 1] = last.astype(jnp.bfloat16)
                    refs = [ref.at[o - 1] for ref in (late_out, late_in, late_send, late_recv)]
                    late[o] = [(send_result(*refs, 0, k), k) for k in range(1, groups)]
                up += cross_sums(theirs, mine, held_select[o - 1][part], width)
            if c < CHUNKS - 1:
                both = jnp.concatenate([down, up], 0).astype(jnp.bfloat16)
                both = lag_terms(inverse[c], both)
                for place, piece in ((reach + o, both[:, :cols]), (reach - o, both[:, cols:])):
                    piece = piece.reshape(groups, share, cols)
                    terms[place] = piece if c == 0 else terms[place] + piece
            else:
                last = lag_terms(inverse[c], up.astype(jnp.bfloat16)).reshape(groups, share, cols)
                back_out[o - 1] = (terms[reach - o] + last).astype(jnp.bfloat16)
                refs = [ref.at[o - 1] for ref in (back_out, back_in, back_send, back_recv)]
                back[o] = [(send_result(*refs, -o, k), k) for k in range(groups)]

    for i, piece in enumerate(pieces[0]):
        if i == 0:
            load_table[0].wait()
        load_records[i].wait()
        whitened[0, block_rows(piece)] = whiten(transform(records[block_rows(piece)], forward[0]))
        if i == 0:
            for later in range(1, CHUNKS):
                load_table[later].start()
            load_inverse.start()
            pl.semaphore_wait(barrier, len(partners))
        send_piece(0, i)
    load_visits.wait()
    for o in range(1, reach + 1):
        copy = pltpu.make_async_remote_copy(
            visits.at[reach - o], held_visits.at[o - 1], visit_send.at[o - 1], visit_recv.at[o - 1],
            device_id=at(o, 0), device_id_type=MESH,
        )
        copy.start()
        send_visits.append(copy)
    for c in range(1, CHUNKS):
        load_table[c].wait()
        for i, piece in enumerate(pieces[c]):
            whitened[c, block_rows(piece)] = whiten(transform(records[block_rows(piece)], forward[c]))
            send_piece(c, i)
    for o in range(reach + 1):
        own_select[o] = selector(visits[reach + o], sets, width)
    load_inverse.wait()
    for c in range(CHUNKS):
        own_visit(c)

    early_out[...] = terms[reach].astype(jnp.bfloat16)
    early = [(send_result(early_out, early_in, early_send, early_recv, 0, k), k) for k in range(1, groups)]

    for o in range(1, reach + 1):
        send_visits[o - 1].wait_recv()
        held_select[o - 1] = selector(held_visits[o - 1], sets, width)

    for c in range(CHUNKS):
        if c == CHUNKS - 1:
            finish(reach, terms[reach, group], early, early_in)
        held_visits_of(c)

    for o in range(1, reach + 1):
        finish(reach + o, terms[reach + o, group], late[o], late_in.at[o - 1])
        finish(reach - o, 0.0, back[o], back_in.at[o - 1])
    for copy in send_visits + list(send_blocks.values()) + send_results:
        copy.wait_send()


def local(records, visits):
    day_local, seg_local, width, samples = records.shape
    visit_count, picks, _ = visits.shape
    days, segs, blocks = lax.axis_size("day"), lax.axis_size("seg"), lax.axis_size("chan")
    reach = blocks // 4
    groups = days * segs
    share = LAGS // groups
    sets = day_local * seg_local
    rows = sets * width
    cols = picks * width
    scale = 1.0 / math.sqrt(FREQS * day_local * days * SEGS)
    bf16, f32 = jnp.bfloat16, jnp.float32
    hbm = pl.BlockSpec(memory_space=pltpu.HBM)
    vmem = pl.BlockSpec(memory_space=pltpu.VMEM)
    dma = pltpu.SemaphoreType.DMA
    flops = 2 * rows * samples * 2 * FREQS + 2 * LAGS * 2 * FREQS * visit_count * cols
    operands = (records.reshape(rows, samples), visits, forward_chunks(samples), inverse_chunks(samples))
    result = pl.pallas_call(
        functools.partial(kernel, (reach, days, segs, blocks, sets, width, picks, scale)),
        out_shape=jax.ShapeDtypeStruct((share, visit_count * cols), bf16),
        in_specs=[hbm, hbm, hbm, hbm],
        out_specs=vmem,
        scratch_shapes=[
            pltpu.VMEM((visit_count, picks, width), jnp.int32),
            pltpu.VMEM((rows, samples), bf16),
            pltpu.VMEM((CHUNKS, samples // 2, 2 * WIDE), bf16),
            pltpu.VMEM((CHUNKS, LAGS, 2 * WIDE), bf16),
            pltpu.VMEM((CHUNKS, rows, 2 * WIDE), bf16),
            pltpu.VMEM((reach, CHUNKS, rows, 2 * WIDE), bf16),
            pltpu.VMEM((reach, picks, width), jnp.int32),
            pltpu.VMEM((reach + 1, sets * cols, rows), bf16),
            pltpu.VMEM((reach, sets * cols, rows), bf16),
            pltpu.VMEM((visit_count, groups, share, cols), f32),
            pltpu.VMEM((groups, share, cols), bf16),
            pltpu.VMEM((reach, groups, share, cols), bf16),
            pltpu.VMEM((reach, groups, share, cols), bf16),
            pltpu.VMEM((groups, share, cols), bf16),
            pltpu.VMEM((reach, groups, share, cols), bf16),
            pltpu.VMEM((reach, groups, share, cols), bf16),
            dma((4,)), dma((CHUNKS,)), dma((reach, CHUNKS, 3)), dma((reach, CHUNKS, 3)), dma((reach,)), dma((reach,)),
            dma((groups,)), dma((groups,)), dma((reach, groups)), dma((reach, groups)),
            dma((reach, groups)), dma((reach, groups)),
        ],
        compiler_params=pltpu.CompilerParams(
            collective_id=0, has_side_effects=True, vmem_limit_bytes=32 * 1024 * 1024
        ),
        cost_estimate=pl.CostEstimate(flops=flops, bytes_accessed=8 * 1024 * 1024, transcendentals=0),
        name="correlate",
    )(*(pltpu.with_memory_space_constraint(jnp.asarray(x), pltpu.HBM) for x in operands))
    return result.reshape(share, visit_count, picks, width)


def solution(mesh):
    in_specs = (P("day", "seg", ("grp", "chan"), None), P(None, None, ("grp", "chan")))
    out_specs = P(("day", "seg"), None, None, ("grp", "chan"))
    return jax.shard_map(local, mesh=mesh, in_specs=in_specs, out_specs=out_specs, check_vma=False)
```

```python
import functools
import math

import jax
import jax.numpy as jnp
import ml_dtypes
import numpy as np
from jax import lax
from jax.experimental import pallas as pl
from jax.experimental.pallas import tpu as pltpu
from jax.sharding import PartitionSpec as P

FREQS = 512
BAND = 64
LAGS = 256
SEGS = 4
WIDE = 128
CHUNKS = FREQS // WIDE
MESH = pl.DeviceIdType.MESH


def forward_chunks(samples):
    index = np.arange(samples // 2)[:, None] * np.arange(FREQS)[None, :] % samples
    turns = index * (2.0 * math.pi / samples)
    table = np.stack([np.cos(turns), -np.sin(turns)], 1).reshape(samples // 2, 2, CHUNKS, WIDE)
    return table.transpose(2, 0, 1, 3).reshape(CHUNKS, samples // 2, 2 * WIDE).astype(ml_dtypes.bfloat16)


def inverse_chunks(samples):
    index = (np.arange(LAGS) - LAGS // 2)[:, None] * np.arange(FREQS)[None, :] % samples
    turns = index * (2.0 * math.pi / samples)
    table = np.stack([np.cos(turns), -np.sin(turns)], 1).reshape(LAGS, 2, CHUNKS, WIDE)
    return table.transpose(2, 0, 1, 3).reshape(CHUNKS, LAGS, 2 * WIDE).astype(ml_dtypes.bfloat16)


def selector(picks, sets, width):
    pick_count = picks.shape[0]
    across = lax.broadcasted_iota(jnp.int32, (width, width), 1)
    down = lax.broadcasted_iota(jnp.int32, (width, width), 0)
    columns = []
    for p in range(pick_count):
        row = picks[p : p + 1, :].astype(jnp.float32)
        diagonal = jnp.where(across == down, jnp.broadcast_to(row, (width, width)), 0.0)
        columns.append(jnp.sum(diagonal, axis=1, keepdims=True))
    column = jnp.concatenate(columns, 0)
    place = lax.broadcasted_iota(jnp.int32, (pick_count * width, sets * width), 1).astype(jnp.float32)
    rows = [jnp.where(place == column + float(s * width), 1.0, 0.0) for s in range(sets)]
    return jnp.concatenate(rows, 0).astype(jnp.bfloat16)


def transform(records, table):
    half = table.shape[0]
    first = jnp.dot(records[:, :half], table, preferred_element_type=jnp.float32)
    second = jnp.dot(records[:, half:], table, preferred_element_type=jnp.float32)
    odd = lax.broadcasted_iota(jnp.int32, first.shape, 1) % 2
    return jnp.where(odd == 1, first - second, first + second)


def whiten(spectra):
    real_part = spectra[:, :WIDE]
    imag_part = spectra[:, WIDE:]
    square = real_part * real_part + imag_part * imag_part
    high = square.astype(jnp.bfloat16)
    low = (square - high.astype(jnp.float32)).astype(jnp.bfloat16)
    down = lax.broadcasted_iota(jnp.int32, (WIDE, WIDE), 0) // BAND
    across = lax.broadcasted_iota(jnp.int32, (WIDE, WIDE), 1) // BAND
    mean = jnp.where(down == across, 0.5 / BAND, 0.0).astype(jnp.bfloat16)
    power = jnp.dot(high, mean, preferred_element_type=jnp.float32)
    power += jnp.dot(low, mean, preferred_element_type=jnp.float32)
    factor = lax.rsqrt(power + 1e-06)
    return jnp.concatenate([real_part * factor, imag_part * factor], 1).astype(jnp.bfloat16)


def cross_sums(own, other, select, width):
    sets = own.shape[0] // width
    picked = jnp.dot(select, other, preferred_element_type=jnp.float32)
    rows = picked.shape[0] // sets
    real_sum = jnp.zeros((rows, WIDE), jnp.float32)
    imag_sum = jnp.zeros((rows, WIDE), jnp.float32)
    for s in range(sets):
        mine = own[s * width : (s + 1) * width].astype(jnp.float32)
        mine = jnp.concatenate([mine] * (rows // width), 0)
        theirs = picked[s * rows : (s + 1) * rows]
        mine_re, mine_im = mine[:, :WIDE], mine[:, WIDE:]
        their_re, their_im = theirs[:, :WIDE], theirs[:, WIDE:]
        real_sum += mine_re * their_re + mine_im * their_im
        imag_sum += mine_re * their_im - mine_im * their_re
    return jnp.concatenate([real_sum, imag_sum], 1)


def lag_terms(table, cross):
    return lax.dot_general(table, cross, (((1,), (1,)), ((), ())), preferred_element_type=jnp.float32)


def kernel(
    dims, records_hbm, visits_hbm, forward_hbm, inverse_hbm, out,
    visits, records, forward, inverse, whitened, held, held_visits, own_select, held_select, terms,
    early_out, late_out, back_out, early_in, late_in, back_in,
    load_sem, table_sem, block_send, block_recv, visit_send, visit_recv,
    early_send, early_recv, late_send, late_recv, back_send, back_recv,
):
    reach, days, segs, blocks, sets, width, picks, scale = dims
    groups = days * segs
    share = LAGS // groups
    cols = picks * width
    chan = lax.axis_index("chan")
    group = lax.axis_index("day") * segs + lax.axis_index("seg")

    def at(offset, step):
        other = lax.rem(group + step, groups)
        return {"chan": lax.rem(chan + offset + blocks, blocks), "day": other // segs, "seg": lax.rem(other, segs)}

    half = sets // 2
    halves = [(0, half), (half, sets - half)] if sets > 1 else [(0, sets)]
    parts = [(0, half), (half, sets - 1 - half), (sets - 1, 1)] if sets > 2 else halves
    pieces = [parts if c == CHUNKS - 1 else halves for c in range(CHUNKS)]

    def block_rows(piece):
        return pl.ds(piece[0] * width, piece[1] * width)

    load_records = [
        pltpu.make_async_copy(records_hbm.at[block_rows(piece)], records.at[block_rows(piece)], load_sem.at[2 + i])
        for i, piece in enumerate(halves)
    ]
    load_inverse = pltpu.make_async_copy(inverse_hbm, inverse, load_sem.at[0])
    load_visits = pltpu.make_async_copy(visits_hbm, visits, load_sem.at[1])
    load_table = [
        pltpu.make_async_copy(forward_hbm.at[c], forward.at[c], table_sem.at[c]) for c in range(CHUNKS)
    ]
    load_table[0].start()
    for copy in load_records:
        copy.start()
    load_visits.start()

    barrier = pltpu.get_barrier_semaphore()
    partners = [(o, k) for o in range(-reach, reach + 1) for k in range(groups) if (o, k) != (0, 0)]
    for o, k in partners:
        pl.semaphore_signal(barrier, inc=1, device_id=at(o, k), device_id_type=MESH)
    send_visits, send_blocks = [], {}

    def send_piece(c, i):
        rows = block_rows(pieces[c][i])
        for o in range(1, reach + 1):
            copy = pltpu.make_async_remote_copy(
                whitened.at[c, rows], held.at[o - 1, c, rows],
                block_send.at[o - 1, c, i], block_recv.at[o - 1, c, i],
                device_id=at(o, 0), device_id_type=MESH,
            )
            copy.start()
            send_blocks[c, o, i] = copy

    def follow(c):
        for place, copy in send_blocks.items():
            if place[0] == c - 2:
                copy.wait_send()
        for i in range(len(pieces[c])):
            send_piece(c, i)

    def own_visit(c):
        mine = whitened[c]
        cross = cross_sums(mine, mine, own_select[0], width).astype(jnp.bfloat16)
        part = lag_terms(inverse[c], cross).reshape(groups, share, cols)
        terms[reach] = part if c == 0 else terms[reach] + part

    send_results = []

    def send_result(source, target, send, recv, offset, step):
        other = lax.rem(group + step, groups)
        copy = pltpu.make_async_remote_copy(
            source.at[other], target.at[step], send.at[step], recv.at[step],
            device_id=at(offset, step), device_id_type=MESH,
        )
        copy.start()
        send_results.append(copy)
        return copy

    def finish(place, total, copies, target):
        for copy, k in copies:
            copy.wait_recv()
            total += target[k].astype(jnp.float32)
        out[:, place * cols : (place + 1) * cols] = (total * scale).astype(jnp.bfloat16)

    back, late = {}, {}

    def held_visits_of(c):
        for o in range(1, reach + 1):
            up, down = 0.0, 0.0
            work = pieces[c] if c == CHUNKS - 1 else [(0, sets)]
            for i, piece in enumerate(work):
                for j in range(len(pieces[c])) if c < CHUNKS - 1 else [i]:
                    send_blocks[c, o, j].wait_recv()
                mine, theirs = whitened[c, block_rows(piece)], held[o - 1, c, block_rows(piece)]
                part = (slice(0, piece[1] * cols), slice(0, piece[1] * width))
                up += cross_sums(theirs, mine, held_select[o - 1][part], width)
                if c == CHUNKS - 1 and i == len(pieces[c]) - 1:
                    last = lag_terms(inverse[c], up.astype(jnp.bfloat16)).reshape(groups, share, cols)
                    back_out[o - 1] = (terms[reach - o] + last).astype(jnp.bfloat16)
                    refs = [ref.at[o - 1] for ref in (back_out, back_in, back_send, back_recv)]
                    back[o] = [(send_result(*refs, -o, k), k) for k in range(groups)]
                down += cross_sums(mine, theirs, own_select[o][part], width)
            if c < CHUNKS - 1:
                both = jnp.concatenate([down, up], 0).astype(jnp.bfloat16)
                both = lag_terms(inverse[c], both)
                for place, piece in ((reach + o, both[:, :cols]), (reach - o, both[:, cols:])):
                    piece = piece.reshape(groups, share, cols)
                    terms[place] = piece if c == 0 else terms[place] + piece
            else:
                last = lag_terms(inverse[c], down.astype(jnp.bfloat16)).reshape(groups, share, cols)
                last += terms[reach + o]
                terms[reach + o] = last
                late_out[o - 1] = last.astype(jnp.bfloat16)
                refs = [ref.at[o - 1] for ref in (late_out, late_in, late_send, late_recv)]
                late[o] = [(send_result(*refs, 0, k), k) for k in range(1, groups)]

    for i, piece in enumerate(pieces[0]):
        if i == 0:
            load_table[0].wait()
        load_records[i].wait()
        whitened[0, block_rows(piece)] = whiten(transform(records[block_rows(piece)], forward[0]))
        if i == 0:
            for later in range(1, CHUNKS):
                load_table[later].start()
            load_inverse.start()
            pl.semaphore_wait(barrier, len(partners))
        send_piece(0, i)
    load_visits.wait()
    for o in range(1, reach + 1):
        copy = pltpu.make_async_remote_copy(
            visits.at[reach - o], held_visits.at[o - 1], visit_send.at[o - 1], visit_recv.at[o - 1],
            device_id=at(o, 0), device_id_type=MESH,
        )
        copy.start()
        send_visits.append(copy)
    for c in range(1, CHUNKS):
        load_table[c].wait()
        for i, piece in enumerate(pieces[c]):
            whitened[c, block_rows(piece)] = whiten(transform(records[block_rows(piece)], forward[c]))
            if c == 1:
                send_piece(c, i)
    for o in range(reach + 1):
        own_select[o] = selector(visits[reach + o], sets, width)
    load_inverse.wait()
    own_visit(0)
    own_visit(1)
    follow(2)
    for c in range(2, CHUNKS):
        own_visit(c)

    early_out[...] = terms[reach].astype(jnp.bfloat16)
    early = [(send_result(early_out, early_in, early_send, early_recv, 0, k), k) for k in range(1, groups)]

    for o in range(1, reach + 1):
        send_visits[o - 1].wait_recv()
        held_select[o - 1] = selector(held_visits[o - 1], sets, width)

    for c in range(CHUNKS):
        if c == CHUNKS - 1:
            finish(reach, terms[reach, group], early, early_in)
        held_visits_of(c)
        if c + 3 < CHUNKS:
            follow(c + 3)

    for o in range(1, reach + 1):
        finish(reach - o, 0.0, back[o], back_in.at[o - 1])
        finish(reach + o, terms[reach + o, group], late[o], late_in.at[o - 1])
    for copy in send_visits + [send_blocks[p] for p in send_blocks if p[0] >= CHUNKS - 2] + send_results:
        copy.wait_send()


def local(records, visits):
    day_local, seg_local, width, samples = records.shape
    visit_count, picks, _ = visits.shape
    days, segs, blocks = lax.axis_size("day"), lax.axis_size("seg"), lax.axis_size("chan")
    reach = blocks // 4
    groups = days * segs
    share = LAGS // groups
    sets = day_local * seg_local
    rows = sets * width
    cols = picks * width
    scale = 1.0 / math.sqrt(FREQS * day_local * days * SEGS)
    bf16, f32 = jnp.bfloat16, jnp.float32
    hbm = pl.BlockSpec(memory_space=pltpu.HBM)
    vmem = pl.BlockSpec(memory_space=pltpu.VMEM)
    dma = pltpu.SemaphoreType.DMA
    flops = 2 * rows * samples * 2 * FREQS + 2 * LAGS * 2 * FREQS * visit_count * cols
    operands = (records.reshape(rows, samples), visits, forward_chunks(samples), inverse_chunks(samples))
    result = pl.pallas_call(
        functools.partial(kernel, (reach, days, segs, blocks, sets, width, picks, scale)),
        out_shape=jax.ShapeDtypeStruct((share, visit_count * cols), bf16),
        in_specs=[hbm, hbm, hbm, hbm],
        out_specs=vmem,
        scratch_shapes=[
            pltpu.VMEM((visit_count, picks, width), jnp.int32),
            pltpu.VMEM((rows, samples), bf16),
            pltpu.VMEM((CHUNKS, samples // 2, 2 * WIDE), bf16),
            pltpu.VMEM((CHUNKS, LAGS, 2 * WIDE), bf16),
            pltpu.VMEM((CHUNKS, rows, 2 * WIDE), bf16),
            pltpu.VMEM((reach, CHUNKS, rows, 2 * WIDE), bf16),
            pltpu.VMEM((reach, picks, width), jnp.int32),
            pltpu.VMEM((reach + 1, sets * cols, rows), bf16),
            pltpu.VMEM((reach, sets * cols, rows), bf16),
            pltpu.VMEM((visit_count, groups, share, cols), f32),
            pltpu.VMEM((groups, share, cols), bf16),
            pltpu.VMEM((reach, groups, share, cols), bf16),
            pltpu.VMEM((reach, groups, share, cols), bf16),
            pltpu.VMEM((groups, share, cols), bf16),
            pltpu.VMEM((reach, groups, share, cols), bf16),
            pltpu.VMEM((reach, groups, share, cols), bf16),
            dma((4,)), dma((CHUNKS,)), dma((reach, CHUNKS, 3)), dma((reach, CHUNKS, 3)), dma((reach,)), dma((reach,)),
            dma((groups,)), dma((groups,)), dma((reach, groups)), dma((reach, groups)),
            dma((reach, groups)), dma((reach, groups)),
        ],
        compiler_params=pltpu.CompilerParams(
            collective_id=0, has_side_effects=True, vmem_limit_bytes=32 * 1024 * 1024
        ),
        cost_estimate=pl.CostEstimate(flops=flops, bytes_accessed=8 * 1024 * 1024, transcendentals=0),
        name="correlate",
    )(*(pltpu.with_memory_space_constraint(jnp.asarray(x), pltpu.HBM) for x in operands))
    return result.reshape(share, visit_count, picks, width)


def solution(mesh):
    in_specs = (P("day", "seg", ("grp", "chan"), None), P(None, None, ("grp", "chan")))
    out_specs = P(("day", "seg"), None, None, ("grp", "chan"))
    return jax.shard_map(local, mesh=mesh, in_specs=in_specs, out_specs=out_specs, check_vma=False)
```

```python
import functools
import math

import jax
import jax.numpy as jnp
import ml_dtypes
import numpy as np
from jax import lax
from jax.experimental import pallas as pl
from jax.experimental.pallas import tpu as pltpu
from jax.sharding import PartitionSpec as P

FREQS = 512
BAND = 64
LAGS = 256
SEGS = 4
WIDE = 128
CHUNKS = FREQS // WIDE
MESH = pl.DeviceIdType.MESH


def forward_chunks(samples):
    index = np.arange(samples // 2)[:, None] * np.arange(FREQS)[None, :] % samples
    turns = index * (2.0 * math.pi / samples)
    table = np.stack([np.cos(turns), -np.sin(turns)], 1).reshape(samples // 2, 2, CHUNKS, WIDE)
    return table.transpose(2, 0, 1, 3).reshape(CHUNKS, samples // 2, 2 * WIDE).astype(ml_dtypes.bfloat16)


def inverse_chunks(samples):
    index = (np.arange(LAGS) - LAGS // 2)[:, None] * np.arange(FREQS)[None, :] % samples
    turns = index * (2.0 * math.pi / samples)
    table = np.stack([np.cos(turns), -np.sin(turns)], 1).reshape(LAGS, 2, CHUNKS, WIDE)
    return table.transpose(2, 0, 1, 3).reshape(CHUNKS, LAGS, 2 * WIDE).astype(ml_dtypes.bfloat16)


def selector(picks, sets, width):
    pick_count = picks.shape[0]
    across = lax.broadcasted_iota(jnp.int32, (width, width), 1)
    down = lax.broadcasted_iota(jnp.int32, (width, width), 0)
    columns = []
    for p in range(pick_count):
        row = picks[p : p + 1, :].astype(jnp.float32)
        diagonal = jnp.where(across == down, jnp.broadcast_to(row, (width, width)), 0.0)
        columns.append(jnp.sum(diagonal, axis=1, keepdims=True))
    column = jnp.concatenate(columns, 0)
    place = lax.broadcasted_iota(jnp.int32, (pick_count * width, sets * width), 1).astype(jnp.float32)
    rows = [jnp.where(place == column + float(s * width), 1.0, 0.0) for s in range(sets)]
    return jnp.concatenate(rows, 0).astype(jnp.bfloat16)


def transform(records, table):
    half = table.shape[0]
    first = jnp.dot(records[:, :half], table, preferred_element_type=jnp.float32)
    second = jnp.dot(records[:, half:], table, preferred_element_type=jnp.float32)
    odd = lax.broadcasted_iota(jnp.int32, first.shape, 1) % 2
    return jnp.where(odd == 1, first - second, first + second)


def whiten(spectra):
    real_part = spectra[:, :WIDE]
    imag_part = spectra[:, WIDE:]
    square = real_part * real_part + imag_part * imag_part
    high = square.astype(jnp.bfloat16)
    low = (square - high.astype(jnp.float32)).astype(jnp.bfloat16)
    down = lax.broadcasted_iota(jnp.int32, (WIDE, WIDE), 0) // BAND
    across = lax.broadcasted_iota(jnp.int32, (WIDE, WIDE), 1) // BAND
    mean = jnp.where(down == across, 0.5 / BAND, 0.0).astype(jnp.bfloat16)
    power = jnp.dot(high, mean, preferred_element_type=jnp.float32)
    power += jnp.dot(low, mean, preferred_element_type=jnp.float32)
    factor = lax.rsqrt(power + 1e-06)
    return jnp.concatenate([real_part * factor, imag_part * factor], 1).astype(jnp.bfloat16)


def cross_sums(own, other, select, width):
    sets = own.shape[0] // width
    picked = jnp.dot(select, other, preferred_element_type=jnp.float32)
    rows = picked.shape[0] // sets
    real_sum = jnp.zeros((rows, WIDE), jnp.float32)
    imag_sum = jnp.zeros((rows, WIDE), jnp.float32)
    for s in range(sets):
        mine = own[s * width : (s + 1) * width].astype(jnp.float32)
        mine = jnp.concatenate([mine] * (rows // width), 0)
        theirs = picked[s * rows : (s + 1) * rows]
        mine_re, mine_im = mine[:, :WIDE], mine[:, WIDE:]
        their_re, their_im = theirs[:, :WIDE], theirs[:, WIDE:]
        real_sum += mine_re * their_re + mine_im * their_im
        imag_sum += mine_re * their_im - mine_im * their_re
    return jnp.concatenate([real_sum, imag_sum], 1)


def lag_terms(table, cross):
    return lax.dot_general(table, cross, (((1,), (1,)), ((), ())), preferred_element_type=jnp.float32)


def kernel(
    dims, records_hbm, visits_hbm, forward_hbm, inverse_hbm, out,
    visits, records, forward, inverse, whitened, held, held_visits, own_select, held_select, terms,
    early_out, late_out, back_out, early_in, late_in, back_in,
    load_sem, table_sem, block_send, block_recv, visit_send, visit_recv,
    early_send, early_recv, late_send, late_recv, back_send, back_recv,
):
    reach, days, segs, blocks, sets, width, picks, scale = dims
    groups = days * segs
    share = LAGS // groups
    cols = picks * width
    chan = lax.axis_index("chan")
    group = lax.axis_index("day") * segs + lax.axis_index("seg")

    def at(offset, step):
        other = lax.rem(group + step, groups)
        return {"chan": lax.rem(chan + offset + blocks, blocks), "day": other // segs, "seg": lax.rem(other, segs)}

    half = sets // 2
    halves = [(0, half), (half, sets - half)] if sets > 1 else [(0, sets)]
    parts = [(0, half), (half, sets - 1 - half), (sets - 1, 1)] if sets > 2 else halves
    pieces = [parts if c == CHUNKS - 1 else halves for c in range(CHUNKS)]

    def block_rows(piece):
        return pl.ds(piece[0] * width, piece[1] * width)

    load_records = [
        pltpu.make_async_copy(records_hbm.at[block_rows(piece)], records.at[block_rows(piece)], load_sem.at[2 + i])
        for i, piece in enumerate(halves)
    ]
    load_inverse = pltpu.make_async_copy(inverse_hbm, inverse, load_sem.at[0])
    load_visits = pltpu.make_async_copy(visits_hbm, visits, load_sem.at[1])
    load_table = [
        pltpu.make_async_copy(forward_hbm.at[c], forward.at[c], table_sem.at[c]) for c in range(CHUNKS)
    ]
    barrier = pltpu.get_barrier_semaphore()
    partners = [(o, k) for o in range(-reach, reach + 1) for k in range(groups) if (o, k) != (0, 0)]
    for o, k in sorted(partners, key=lambda p: p[1] != 0):
        pl.semaphore_signal(barrier, inc=1, device_id=at(o, k), device_id_type=MESH)
    load_table[0].start()
    for copy in load_records:
        copy.start()
    load_visits.start()

    send_visits, send_blocks = [], {}

    def send_piece(c, i):
        rows = block_rows(pieces[c][i])
        for o in range(1, reach + 1):
            copy = pltpu.make_async_remote_copy(
                whitened.at[c, rows], held.at[o - 1, c, rows],
                block_send.at[o - 1, c, i], block_recv.at[o - 1, c, i],
                device_id=at(o, 0), device_id_type=MESH,
            )
            copy.start()
            send_blocks[c, o, i] = copy

    def follow(c):
        for place, copy in send_blocks.items():
            if place[0] == c - 2:
                copy.wait_send()
        for i in range(len(pieces[c])):
            send_piece(c, i)

    def own_visit(c):
        mine = whitened[c]
        cross = cross_sums(mine, mine, own_select[0], width).astype(jnp.bfloat16)
        part = lag_terms(inverse[c], cross).reshape(groups, share, cols)
        terms[reach] = part if c == 0 else terms[reach] + part

    send_results = []

    def send_result(source, target, send, recv, offset, step):
        other = lax.rem(group + step, groups)
        copy = pltpu.make_async_remote_copy(
            source.at[other], target.at[step], send.at[step], recv.at[step],
            device_id=at(offset, step), device_id_type=MESH,
        )
        copy.start()
        send_results.append(copy)
        return copy

    def finish(place, total, copies, target):
        for copy, k in copies:
            copy.wait_recv()
            total += target[k].astype(jnp.float32)
        out[:, place * cols : (place + 1) * cols] = (total * scale).astype(jnp.bfloat16)

    back, late = {}, {}

    def held_visits_of(c):
        for o in range(1, reach + 1):
            up, down = 0.0, 0.0
            work = pieces[c] if c == CHUNKS - 1 else [(0, sets)]
            for i, piece in enumerate(work):
                for j in range(len(pieces[c])) if c < CHUNKS - 1 else [i]:
                    send_blocks[c, o, j].wait_recv()
                mine, theirs = whitened[c, block_rows(piece)], held[o - 1, c, block_rows(piece)]
                part = (slice(0, piece[1] * cols), slice(0, piece[1] * width))
                up += cross_sums(theirs, mine, held_select[o - 1][part], width)
                if c == CHUNKS - 1 and i == len(pieces[c]) - 1:
                    last = lag_terms(inverse[c], up.astype(jnp.bfloat16)).reshape(groups, share, cols)
                    back_out[o - 1] = (terms[reach - o] + last).astype(jnp.bfloat16)
                    refs = [ref.at[o - 1] for ref in (back_out, back_in, back_send, back_recv)]
                    back[o] = [(send_result(*refs, -o, k), k) for k in range(groups)]
                down += cross_sums(mine, theirs, own_select[o][part], width)
            if c < CHUNKS - 1:
                both = jnp.concatenate([down, up], 0).astype(jnp.bfloat16)
                both = lag_terms(inverse[c], both)
                for place, piece in ((reach + o, both[:, :cols]), (reach - o, both[:, cols:])):
                    piece = piece.reshape(groups, share, cols)
                    terms[place] = piece if c == 0 else terms[place] + piece
            else:
                last = lag_terms(inverse[c], down.astype(jnp.bfloat16)).reshape(groups, share, cols)
                last += terms[reach + o]
                terms[reach + o] = last
                late_out[o - 1] = last.astype(jnp.bfloat16)
                refs = [ref.at[o - 1] for ref in (late_out, late_in, late_send, late_recv)]
                late[o] = [(send_result(*refs, 0, k), k) for k in range(1, groups)]

    for i, piece in enumerate(pieces[0]):
        if i == 0:
            load_table[0].wait()
        load_records[i].wait()
        whitened[0, block_rows(piece)] = whiten(transform(records[block_rows(piece)], forward[0]))
        if i == 0:
            for later in range(1, CHUNKS):
                load_table[later].start()
            load_inverse.start()
            pl.semaphore_wait(barrier, len(partners))
        send_piece(0, i)
    load_visits.wait()
    for o in range(1, reach + 1):
        copy = pltpu.make_async_remote_copy(
            visits.at[reach - o], held_visits.at[o - 1], visit_send.at[o - 1], visit_recv.at[o - 1],
            device_id=at(o, 0), device_id_type=MESH,
        )
        copy.start()
        send_visits.append(copy)
    for c in range(1, CHUNKS):
        load_table[c].wait()
        for i, piece in enumerate(pieces[c]):
            whitened[c, block_rows(piece)] = whiten(transform(records[block_rows(piece)], forward[c]))
            if c == 1:
                send_piece(c, i)
    for o in range(reach + 1):
        own_select[o] = selector(visits[reach + o], sets, width)
    load_inverse.wait()
    own_visit(0)
    own_visit(1)
    follow(2)
    for c in range(2, CHUNKS):
        own_visit(c)

    early_out[...] = terms[reach].astype(jnp.bfloat16)
    early = [(send_result(early_out, early_in, early_send, early_recv, 0, k), k) for k in range(1, groups)]

    for o in range(1, reach + 1):
        send_visits[o - 1].wait_recv()
        held_select[o - 1] = selector(held_visits[o - 1], sets, width)

    for c in range(CHUNKS):
        if c == CHUNKS - 1:
            finish(reach, terms[reach, group], early, early_in)
        held_visits_of(c)
        if c + 3 < CHUNKS:
            follow(c + 3)

    for o in range(1, reach + 1):
        finish(reach - o, 0.0, back[o], back_in.at[o - 1])
        finish(reach + o, terms[reach + o, group], late[o], late_in.at[o - 1])
    for copy in send_visits + [send_blocks[p] for p in send_blocks if p[0] >= CHUNKS - 2] + send_results:
        copy.wait_send()


def local(records, visits):
    day_local, seg_local, width, samples = records.shape
    visit_count, picks, _ = visits.shape
    days, segs, blocks = lax.axis_size("day"), lax.axis_size("seg"), lax.axis_size("chan")
    reach = blocks // 4
    groups = days * segs
    share = LAGS // groups
    sets = day_local * seg_local
    rows = sets * width
    cols = picks * width
    scale = 1.0 / math.sqrt(FREQS * day_local * days * SEGS)
    bf16, f32 = jnp.bfloat16, jnp.float32
    hbm = pl.BlockSpec(memory_space=pltpu.HBM)
    vmem = pl.BlockSpec(memory_space=pltpu.VMEM)
    dma = pltpu.SemaphoreType.DMA
    flops = 2 * rows * samples * 2 * FREQS + 2 * LAGS * 2 * FREQS * visit_count * cols
    operands = (records.reshape(rows, samples), visits, forward_chunks(samples), inverse_chunks(samples))
    result = pl.pallas_call(
        functools.partial(kernel, (reach, days, segs, blocks, sets, width, picks, scale)),
        out_shape=jax.ShapeDtypeStruct((share, visit_count * cols), bf16),
        in_specs=[hbm, hbm, hbm, hbm],
        out_specs=vmem,
        scratch_shapes=[
            pltpu.VMEM((visit_count, picks, width), jnp.int32),
            pltpu.VMEM((rows, samples), bf16),
            pltpu.VMEM((CHUNKS, samples // 2, 2 * WIDE), bf16),
            pltpu.VMEM((CHUNKS, LAGS, 2 * WIDE), bf16),
            pltpu.VMEM((CHUNKS, rows, 2 * WIDE), bf16),
            pltpu.VMEM((reach, CHUNKS, rows, 2 * WIDE), bf16),
            pltpu.VMEM((reach, picks, width), jnp.int32),
            pltpu.VMEM((reach + 1, sets * cols, rows), bf16),
            pltpu.VMEM((reach, sets * cols, rows), bf16),
            pltpu.VMEM((visit_count, groups, share, cols), f32),
            pltpu.VMEM((groups, share, cols), bf16),
            pltpu.VMEM((reach, groups, share, cols), bf16),
            pltpu.VMEM((reach, groups, share, cols), bf16),
            pltpu.VMEM((groups, share, cols), bf16),
            pltpu.VMEM((reach, groups, share, cols), bf16),
            pltpu.VMEM((reach, groups, share, cols), bf16),
            dma((4,)), dma((CHUNKS,)), dma((reach, CHUNKS, 3)), dma((reach, CHUNKS, 3)), dma((reach,)), dma((reach,)),
            dma((groups,)), dma((groups,)), dma((reach, groups)), dma((reach, groups)),
            dma((reach, groups)), dma((reach, groups)),
        ],
        compiler_params=pltpu.CompilerParams(
            collective_id=0, has_side_effects=True, vmem_limit_bytes=32 * 1024 * 1024
        ),
        cost_estimate=pl.CostEstimate(flops=flops, bytes_accessed=8 * 1024 * 1024, transcendentals=0),
        name="correlate",
    )(*(pltpu.with_memory_space_constraint(jnp.asarray(x), pltpu.HBM) for x in operands))
    return result.reshape(share, visit_count, picks, width)


def solution(mesh):
    in_specs = (P("day", "seg", ("grp", "chan"), None), P(None, None, ("grp", "chan")))
    out_specs = P(("day", "seg"), None, None, ("grp", "chan"))
    return jax.shard_map(local, mesh=mesh, in_specs=in_specs, out_specs=out_specs, check_vma=False)
```
